32 devices in a mesh: layer: 4 (over z), plane: 8 (over y, x, core).
Axes of the slice: x: 2, y: 2, z: 4, core: 2. Of those that a mesh axis runs over, the one named last changes fastest.
Arguments:
- leaf_rhs: bfloat16 [256, 128, 512], P(('layer', 'plane')), may hold values from -6 to 6
- leaf_inverse: bfloat16 [256, 128, 128], P(('layer', 'plane')), may hold values from -0.5 to 0.5
- leaf_couple: bfloat16 [256, 2, 1024, 128], P(('layer', 'plane')), may hold values from -0.09375 to 0.09375
- couple_mask: int32 [256, 2], P(('layer', 'plane')), may hold values 0 or 1
- leaf_diag: float32 [256, 128], P(('layer', 'plane')), may hold values from 0.5 to 2
- sep_rhs: bfloat16 [3, 1024, 512], P(None, 'plane'), may hold values from -6 to 6
- sep_inverse: bfloat16 [3, 1024, 1024], P(None, 'plane'), may hold values from -0.1875 to 0.1875
- sep_couple: bfloat16 [3, 1, 1024, 1024], P(None, None, 'plane'), may hold values from -0.125 to 0.125
- sep_diag: float32 [3, 1024], P(None, 'plane'), may hold values from 0.5 to 2
Outputs:
- leaf_solution: bfloat16 [256, 128, 512], P(('layer', 'plane'))
- sep_solution: bfloat16 [4, 2, 1024, 512], P('layer', None, 'plane')
The draws below stay inside these ranges and needn't reach their ends.
All inputs are finite; a program needn't handle non-finite values. No bound on the sum of `couple_mask` on one device may be relied on, other than what follows from the above.
Results may differ from the reference program's by a relative error of at most 0.02.
Values may be sent and summed in bfloat16 or wider, within the bound.
No kernel may reach another device: no remote copies, remote signals or barrier semaphores. Data moves between devices by JAX's collectives and lax.ppermute only.
A program may use at most 128 MiB of HBM per device.

```python
import math
import jax
import jax.numpy as jnp
from jax import lax

BLK = 128
SEP = 1024
RHS = 512
LB = 8
LEVELS = 2
NSEP = 3
NBLOCKS = 256
N_LAYER = 4
N_PLANE = 8


def plant(array, own_key, smallest, top_value):
    place = [jax.random.randint(jax.random.fold_in(own_key, axis), (), 0, length) for axis, length in enumerate(array.shape)]
    main_axis = array.shape.index(max(array.shape))
    neighbour = place[:main_axis] + [(place[main_axis] + 1) % array.shape[main_axis]] + place[main_axis + 1:]
    return array.at[tuple(place)].set(smallest).at[tuple(neighbour)].set(top_value)


def strengthened(array, own_key, source, target, parts, factor):
    owner, partner = [(jnp.arange(array.shape[axis_at]) // (array.shape[axis_at] // parts)).reshape([-1 if axis == axis_at else 1 for axis in range(array.ndim)]) for axis_at in (source, target)]
    chosen = jax.random.permutation(own_key, parts)[partner]
    strong = (owner == chosen) | (owner == (partner + parts // 2) % parts)
    return jnp.where(strong, factor * array, array)


def level_of(key, dims, split, smallest, largest):
    def one(position, blocks):
        steps = jax.random.uniform(jax.random.fold_in(jax.random.fold_in(key, 6), position), (blocks,), jnp.float32, smallest / len(split), largest / len(split))
        return jnp.repeat(jnp.exp(steps), dims[position] // blocks).reshape((-1,) + (1,) * (len(dims) - position - 1))

    factor_of = one(*split[0])
    for cut in split[1:]:
        factor_of = factor_of * one(*cut)
    return factor_of


def scatter_about(key, shape, width, limit, cuts=(), held_as=jnp.bfloat16):
    result = jax.random.normal(key, shape, jnp.float32) * width
    if len(cuts) > 0:
        result = level_of(key, shape, cuts, -0.22, 0.18) * result
    return jnp.clip(result, min=-limit, max=limit).astype(held_as)


def heavy_noise(rng, shape, spread, bound, cuts, heavy, dtype=jnp.bfloat16):
    result = spread * jax.random.normal(rng, shape, jnp.float32)
    if cuts:
        result = result * level_of(rng, shape, cuts, -0.22, 0.18)
    return jnp.clip(strengthened(result, jax.random.fold_in(rng, 3), *heavy), -bound, bound).astype(dtype)


def setup_inputs(seed: int = 0) -> dict:
    streams_of = jax.random.split(jax.random.key(seed), 10)
    leaf_rhs = scatter_about(streams_of[0], (NBLOCKS, BLK, RHS), 1.0, 6.0, ((0, 32),))
    leaf_inverse = scatter_about(streams_of[1], (NBLOCKS, BLK, BLK), BLK ** -0.5, 0.5, ((0, 32),))
    leaf_couple = heavy_noise(streams_of[2], (NBLOCKS, LEVELS, SEP, BLK), (LB * BLK * N_PLANE * 2) ** -0.5, 0.09375, ((0, 32),), (0, 2, 32, 2.75))
    couple_mask = plant((jax.random.randint(streams_of[3], (NBLOCKS, LEVELS), 0, 4) < 3).astype(jnp.int32), jax.random.fold_in(streams_of[3], 1), 0, 1)
    leaf_diag = jnp.clip(jnp.exp(math.log(2.0) - 1.3862944 * jax.random.uniform(streams_of[4], (NBLOCKS, BLK), jnp.float32) ** level_of(streams_of[4], (NBLOCKS, BLK), ((0, 32),), -0.2, 0.2)), 0.5, 2.0)
    sep_rhs = scatter_about(streams_of[5], (NSEP, SEP, RHS), 1.0, 6.0, ((1, 8),))
    sep_inverse = scatter_about(streams_of[6], (NSEP, SEP, SEP), SEP ** -0.5, 0.1875, ((1, 8),))
    sep_couple = scatter_about(streams_of[7], (NSEP, LEVELS - 1, SEP, SEP), (SEP * 2) ** -0.5, 0.125, ((2, 8),))
    sep_diag = jnp.clip(jnp.exp(math.log(2.0) - 1.3862944 * jax.random.uniform(streams_of[8], (NSEP, SEP), jnp.float32) ** level_of(streams_of[8], (NSEP, SEP), ((1, 8),), -0.2, 0.2)), 0.5, 2.0)
    return dict(leaf_rhs=leaf_rhs, leaf_inverse=leaf_inverse, leaf_couple=leaf_couple, couple_mask=couple_mask, leaf_diag=leaf_diag, sep_rhs=sep_rhs, sep_inverse=sep_inverse, sep_couple=sep_couple, sep_diag=sep_diag)


def lower_unit(block, first_row):
    row_count = block.shape[-2]
    col_count = block.shape[-1]
    row_ids = first_row + lax.broadcasted_iota(jnp.int32, (row_count, col_count), 0)
    col_ids = lax.broadcasted_iota(jnp.int32, (row_count, col_count), 1)
    below = jnp.where(col_ids < row_ids, block, jnp.zeros_like(block))
    return jnp.where(col_ids == row_ids, jnp.ones_like(block), below)


def reference(leaf_rhs, leaf_inverse, leaf_couple, couple_mask, leaf_diag, sep_rhs, sep_inverse, sep_couple, sep_diag):
    per_layer = N_PLANE * LB
    leaf_values = []
    leaf_terms = []
    for layer_id in range(N_LAYER):
        first = layer_id * per_layer
        lower_part = lower_unit(leaf_inverse[first:first + per_layer], 0).astype(jnp.float32)
        solved = jnp.einsum("bij,bjr->bir", lower_part, leaf_rhs[first:first + per_layer].astype(jnp.float32)).astype(jnp.bfloat16)
        masked = leaf_couple[first:first + per_layer].astype(jnp.float32) * couple_mask[first:first + per_layer].astype(jnp.float32)[:, :, None, None]
        leaf_terms.append(jnp.einsum("bksc,bcr->ksr", masked, solved.astype(jnp.float32)))
        leaf_values.append(solved)
    group_sums = jnp.stack(leaf_terms)
    sep_z = []
    for level in range(1, LEVELS + 1):
        group_sums = group_sums[0::2] + group_sums[1::2]
        count_here = N_LAYER >> level
        offset = N_LAYER - 2 * count_here
        residual = (sep_rhs[offset:offset + count_here].astype(jnp.float32) - group_sums[:, level - 1]).astype(jnp.bfloat16)
        lower_part = lower_unit(sep_inverse[offset:offset + count_here], 0).astype(jnp.float32)
        solved = jnp.einsum("gij,gjr->gir", lower_part, residual.astype(jnp.float32)).astype(jnp.bfloat16)
        if level < LEVELS:
            blocks = sep_couple[offset:offset + count_here, :LEVELS - level].astype(jnp.float32)
            coupling = jnp.einsum("gjts,gsr->gjtr", blocks, solved.astype(jnp.float32))
            group_sums = group_sums.at[:, level:].add(coupling)
        sep_z.append(solved.astype(jnp.float32) / sep_diag[offset:offset + count_here][:, :, None])
    sep_x = [None] * LEVELS
    for level in range(LEVELS, 0, -1):
        count_here = N_LAYER >> level
        offset = N_LAYER - 2 * count_here
        target_now = sep_z[level - 1]
        if level < LEVELS:
            blocks = sep_couple[offset:offset + count_here, :LEVELS - level].astype(jnp.float32)
            carried = jnp.zeros(target_now.shape, jnp.float32)
            for slot in range(LEVELS - level):
                upper_level = level + 1 + slot
                upper_rows = jnp.repeat(sep_x[upper_level - 1], 2 ** (upper_level - level), axis=0)
                carried = carried + jnp.einsum("gts,gtr->gsr", blocks[:, slot], upper_rows.astype(jnp.float32))
            target_now = target_now - carried
        target_now = target_now.astype(jnp.bfloat16)
        lower_part = lower_unit(sep_inverse[offset:offset + count_here], 0).astype(jnp.float32)
        sep_x[level - 1] = jnp.einsum("gts,gtr->gsr", lower_part, target_now.astype(jnp.float32)).astype(jnp.bfloat16)
    sep_solution = jnp.stack([jnp.repeat(sep_x[level - 1], 2 ** level, axis=0) for level in range(1, LEVELS + 1)], axis=1)
    leaf_outputs = []
    for layer_id in range(N_LAYER):
        first = layer_id * per_layer
        above = jnp.stack([sep_x[level - 1][layer_id >> level] for level in range(1, LEVELS + 1)]).astype(jnp.float32)
        masked = leaf_couple[first:first + per_layer].astype(jnp.float32) * couple_mask[first:first + per_layer].astype(jnp.float32)[:, :, None, None]
        back_terms = jnp.einsum("bksc,ksr->bcr", masked, above)
        leaf_target = (leaf_values[layer_id].astype(jnp.float32) / leaf_diag[first:first + per_layer][:, :, None] - back_terms).astype(jnp.bfloat16)
        lower_part = lower_unit(leaf_inverse[first:first + per_layer], 0).astype(jnp.float32)
        leaf_outputs.append(jnp.einsum("bjc,bjr->bcr", lower_part, leaf_target.astype(jnp.float32)).astype(jnp.bfloat16))
    return jnp.concatenate(leaf_outputs, axis=0), sep_solution
```

```python
import jax
import jax.numpy as jnp
import numpy as np
from jax import lax
from jax.sharding import PartitionSpec as P

F32 = jnp.float32
BF16 = jnp.bfloat16


def bit_orders(planes):
    link_bits = list(range(1, planes.bit_length() - 1))
    turn = len(link_bits) // 2
    return [link_bits, link_bits[turn:] + link_bits[:turn]]


def slot_table(planes):
    orders = bit_orders(planes)
    count = len(orders[0])
    table = np.zeros((planes, planes), np.int32)
    for device in range(planes):
        for slot in range(planes):
            other = slot >> count
            order = orders[(device & 1) ^ other]
            block = device ^ other
            for place, bit in enumerate(order):
                if slot >> (count - 1 - place) & 1:
                    block ^= 1 << bit
            table[device, slot] = block
    return table


def swap_core(value):
    planes = lax.axis_size("plane")
    return lax.ppermute(value, "plane", [(i, i ^ 1) for i in range(planes)])


def swap_link(value, place):
    planes = lax.axis_size("plane")
    orders = bit_orders(planes)
    return lax.ppermute(value, "plane", [(i, i ^ (1 << orders[i & 1][place])) for i in range(planes)])


def swap_layer(value, stride):
    layers = lax.axis_size("layer")
    return lax.ppermute(value, "layer", [(i, i ^ (1 << stride)) for i in range(layers)])


def scatter_sum(value):
    planes = lax.axis_size("plane")
    half = planes // 2
    value = (value[:half].astype(F32) + swap_core(value[half:]).astype(F32)).astype(BF16)
    for place in range(len(bit_orders(planes)[0])):
        half //= 2
        value = (value[:half].astype(F32) + swap_link(value[half:], place).astype(F32)).astype(BF16)
    return value[0]


def gather(value):
    planes = lax.axis_size("plane")
    value = value[None]
    for place in reversed(range(len(bit_orders(planes)[0]))):
        value = jnp.concatenate([value, swap_link(value, place)], axis=0)
    return jnp.concatenate([value, swap_core(value)], axis=0)


def reorder(value, indices, axis):
    pieces = [
        lax.dynamic_index_in_dim(value, indices[i], axis, keepdims=True)
        for i in range(value.shape[axis])
    ]
    return jnp.concatenate(pieces, axis=axis)


def lower_unit(block, first_row):
    row_count = block.shape[-2]
    col_count = block.shape[-1]
    row_ids = first_row + lax.broadcasted_iota(jnp.int32, (row_count, col_count), 0)
    col_ids = lax.broadcasted_iota(jnp.int32, (row_count, col_count), 1)
    below = jnp.where(col_ids < row_ids, block, jnp.zeros_like(block))
    return jnp.where(col_ids == row_ids, jnp.ones_like(block), below)


def body(
    leaf_rhs,
    leaf_inverse,
    leaf_couple,
    couple_mask,
    leaf_diag,
    sep_rhs,
    sep_inverse,
    sep_couple,
    sep_diag,
):
    levels = leaf_couple.shape[1]
    planes = lax.axis_size("plane")
    layers = lax.axis_size("layer")
    own_rows = sep_rhs.shape[1]
    sep_rows = own_rows * planes
    rhs_cols = sep_rhs.shape[2]
    cols = rhs_cols // planes
    layer_id = lax.axis_index("layer")
    me = lax.axis_index("plane")
    first_row = me * own_rows
    table = slot_table(planes)
    inverse_table = np.argsort(table, axis=1).astype(np.int32)
    slot_block = lax.dynamic_index_in_dim(jnp.asarray(table), me, 0, keepdims=False)
    block_slot = lax.dynamic_index_in_dim(jnp.asarray(inverse_table), me, 0, keepdims=False)
    sep_ids = [
        layers - (layers >> level - 1) + jnp.right_shift(layer_id, level)
        for level in range(1, levels + 1)
    ]

    def select_sep(array, level):
        return lax.dynamic_index_in_dim(array, sep_ids[level - 1], 0, keepdims=False)

    mats = []
    for level in range(1, levels + 1):
        mats.append(lower_unit(select_sep(sep_inverse, level), first_row)[None])
        if level < levels:
            mats.append(select_sep(sep_couple, level)[: levels - level])
    sizes = [m.shape[0] for m in mats]
    full = gather(jnp.concatenate(mats, axis=0))
    inverses, couples, at = [], [], 0
    for level in range(1, levels + 1):
        inverses.append(full[:, at])
        at += 1
        if level < levels:
            couples.append(full[:, at : at + levels - level])
            at += levels - level
    diag_full = lax.all_gather(sep_diag, "plane", axis=1, tiled=True)

    leaf_lower = lower_unit(leaf_inverse, 0)
    leaf_y = jnp.einsum("bij,bjr->rbi", leaf_lower, leaf_rhs, preferred_element_type=F32).astype(BF16)
    masked = leaf_couple * couple_mask.astype(BF16)[:, :, None, None]
    partial = jnp.einsum("rbc,bksc->rks", leaf_y, masked, preferred_element_type=F32)
    partial = partial.reshape(planes, cols, levels, planes, own_rows)
    for level in range(1, levels + 1):
        first = (jnp.bitwise_and(layer_id, (1 << level) - 1) == 0).astype(F32)
        term = select_sep(sep_rhs, level).astype(F32).T.reshape(planes, cols, own_rows) * first
        chosen = (jnp.arange(planes) == me).astype(F32)
        partial = partial.at[:, :, level - 1].add(-term[:, :, None, :] * chosen[:, None])
    partial = partial.astype(BF16).reshape(planes, cols, levels, sep_rows)
    partial = reorder(partial, slot_block, 0)
    sums = scatter_sum(partial).astype(F32)
    sums = [sums[:, level] for level in range(levels)]

    def rows_times(matrix, vector):
        out = jnp.einsum("rs,pos->rpo", vector, matrix, preferred_element_type=F32)
        return reorder(out, block_slot, 1).reshape(cols, sep_rows)

    def times_rows(vector, matrix):
        parts = reorder(vector.reshape(cols, planes, own_rows), slot_block, 1)
        return jnp.einsum("rpo,pos->rs", parts, matrix, preferred_element_type=F32)

    sep_z = []
    for level in range(1, levels + 1):
        for upper in range(level - 1, levels):
            theirs = swap_layer(sums[upper].astype(BF16), level - 1).astype(F32)
            sums[upper] = sums[upper] + theirs
        residual = (-sums[level - 1]).astype(BF16)
        solved = rows_times(inverses[level - 1], residual).astype(BF16)
        for slot in range(levels - level):
            sums[level + slot] = sums[level + slot] + rows_times(couples[level - 1][:, slot], solved)
        sep_z.append(solved.astype(F32) / select_sep(diag_full, level)[None])
    answers = [None] * levels
    everywhere = [None] * levels
    for level in range(levels, 0, -1):
        target = sep_z[level - 1]
        for slot in range(levels - level):
            target = target - times_rows(answers[level + slot], couples[level - 1][:, slot])
        answers[level - 1] = times_rows(target.astype(BF16), inverses[level - 1]).astype(BF16)
        everywhere[level - 1] = gather(answers[level - 1])

    above = reorder(jnp.stack(everywhere, axis=2), block_slot, 0).reshape(rhs_cols, levels, sep_rows)
    back = jnp.einsum("rks,bksc->rbc", above, masked, preferred_element_type=F32)
    target = (leaf_y.astype(F32) / leaf_diag[None] - back).astype(BF16)
    leaf_solution = jnp.einsum("bjc,rbj->bcr", leaf_lower, target, preferred_element_type=F32).astype(BF16)
    mine = lax.dynamic_slice_in_dim(above, first_row, own_rows, 2)
    sep_solution = jnp.transpose(mine, (1, 2, 0))[None]
    return (leaf_solution, sep_solution)


def solution(mesh):
    in_specs = (
        P(("layer", "plane"), None, None),
        P(("layer", "plane"), None, None),
        P(("layer", "plane"), None, None, None),
        P(("layer", "plane"), None),
        P(("layer", "plane"), None),
        P(None, "plane", None),
        P(None, "plane", None),
        P(None, None, "plane", None),
        P(None, "plane"),
    )
    out_specs = (P(("layer", "plane"), None, None), P("layer", None, "plane", None))
    return jax.shard_map(body, mesh=mesh, in_specs=in_specs, out_specs=out_specs, check_vma=False)
```

```python
import jax
import jax.numpy as jnp
import numpy as np
from jax import lax
from jax.experimental import pallas as pl
from jax.experimental.pallas import tpu as pltpu
from jax.sharding import PartitionSpec as P

F32 = jnp.float32
BF16 = jnp.bfloat16
LANES = 128
TILE = 256
DIAG_ROWS = 16
NT = (((1,), (1,)), ((), ()))
VMEM = pltpu.CompilerParams(vmem_limit_bytes=32 * 1024 * 1024)


def bit_orders(planes):
    link_bits = list(range(1, planes.bit_length() - 1))
    turn = len(link_bits) // 2
    return [link_bits, link_bits[turn:] + link_bits[:turn]]


def slot_table(planes):
    orders = bit_orders(planes)
    count = len(orders[0])
    table = np.zeros((planes, planes), np.int32)
    for device in range(planes):
        for slot in range(planes):
            other = slot >> count
            order = orders[(device & 1) ^ other]
            block = device ^ other
            for place, bit in enumerate(order):
                if slot >> (count - 1 - place) & 1:
                    block ^= 1 << bit
            table[device, slot] = block
    return table


def swap_core(value):
    planes = lax.axis_size("plane")
    return lax.ppermute(value, "plane", [(i, i ^ 1) for i in range(planes)])


def swap_link(value, place):
    planes = lax.axis_size("plane")
    orders = bit_orders(planes)
    return lax.ppermute(value, "plane", [(i, i ^ (1 << orders[i & 1][place])) for i in range(planes)])


def swap_layer(value, stride):
    layers = lax.axis_size("layer")
    return lax.ppermute(value, "layer", [(i, i ^ (1 << stride)) for i in range(layers)])


def added(*terms):
    total = terms[0].astype(F32)
    for term in terms[1:]:
        total = total + term.astype(F32)
    return total.astype(BF16)


def scatter_sum(keep, send):
    places = len(bit_orders(lax.axis_size("plane"))[0])
    terms = [keep, swap_core(send)]
    for place in range(places):
        half = terms[0].shape[0] // 2
        theirs = swap_link(added(*[term[half:] for term in terms]), place)
        terms = [term[:half] for term in terms] + [theirs]
    return added(*[term[0] for term in terms])


def gather(value):
    pieces = [value]
    for place in reversed(range(len(bit_orders(lax.axis_size("plane"))[0]))):
        pieces = pieces + [swap_link(piece, place) for piece in pieces]
    return pieces + [swap_core(piece) for piece in pieces]


def lower_unit(block, first_row):
    row_count = block.shape[-2]
    col_count = block.shape[-1]
    row_ids = first_row + lax.broadcasted_iota(jnp.int32, (row_count, col_count), 0)
    col_ids = lax.broadcasted_iota(jnp.int32, (row_count, col_count), 1)
    below = jnp.where(col_ids < row_ids, block, jnp.zeros_like(block))
    return jnp.where(col_ids == row_ids, jnp.ones_like(block), below)


def nt(left, right):
    return lax.dot_general(left, right, NT, preferred_element_type=F32)


def nn(left, right):
    return jnp.dot(left, right, preferred_element_type=F32)


ME, LAYER, SLOTS = 0, 1, 2


def collect_call(info, sep_inverse, sep_couple, sep_diag, levels, layers):
    own_rows, sep_rows = sep_inverse.shape[1:]

    def sep_id(info, level):
        return layers - (layers >> level - 1) + jnp.right_shift(info[LAYER], level)

    def kernel(info, *refs):
        inverse, couple = refs[:levels], refs[levels : 2 * levels - 1]
        diag = refs[2 * levels - 1]
        outs = refs[2 * levels :]
        for level in range(1, levels + 1):
            out = outs[level - 1]
            out[:own_rows] = lower_unit(inverse[level - 1][0].astype(F32), info[ME] * own_rows).astype(BF16)
            for slot in range(levels - level):
                out[(slot + 1) * own_rows : (slot + 2) * own_rows] = couple[level - 1][0, slot]
        rows = []
        for level in range(1, levels + 1):
            value = diag[pl.ds(sep_id(info, level), 1)]
            high = value.astype(BF16).astype(F32)
            rows += [high, value - high]
        rows.append(jnp.zeros((DIAG_ROWS - len(rows), own_rows), F32))
        last = outs[-1]
        last[own_rows:] = jnp.zeros((DIAG_ROWS, sep_rows), BF16)
        last[own_rows:, :own_rows] = jnp.concatenate(rows, axis=0).astype(BF16)

    specs = [
        pl.BlockSpec((1, own_rows, sep_rows), lambda i, info, level=level: (sep_id(info, level), 0, 0))
        for level in range(1, levels + 1)
    ]
    specs += [
        pl.BlockSpec(
            (1, sep_couple.shape[1], own_rows, sep_rows),
            lambda i, info, level=level: (sep_id(info, level), 0, 0, 0),
        )
        for level in range(1, levels)
    ]
    specs.append(pl.BlockSpec(sep_diag.shape, lambda i, info: (0, 0)))
    shapes = [((1 + levels - level) * own_rows, sep_rows) for level in range(1, levels + 1)]
    shapes[-1] = (own_rows + DIAG_ROWS, sep_rows)
    return pl.pallas_call(
        kernel,
        grid_spec=pltpu.PrefetchScalarGridSpec(
            num_scalar_prefetch=1,
            grid=(1,),
            in_specs=specs,
            out_specs=[pl.BlockSpec(shape, lambda i, info: (0, 0)) for shape in shapes],
        ),
        out_shape=[jax.ShapeDtypeStruct(shape, BF16) for shape in shapes],
        compiler_params=VMEM,
        name="collect",
    )(info, *([sep_inverse] * levels), *([sep_couple] * (levels - 1)), sep_diag)


def leaf_forward_call(info, mask, leaves, couple, sep_rhs, level, layers):
    first = level == 1
    blocks, _, sep_rows, block_rows = couple.shape
    own_rows, rhs_cols = sep_rhs.shape[1:]
    planes = sep_rows // own_rows
    half, cols = planes // 2, rhs_cols // planes
    width = blocks * block_rows
    tile = min(TILE, sep_rows)

    def sep_id(info):
        return layers - (layers >> level - 1) + jnp.right_shift(info[LAYER], level)

    def kernel(info, mask, *refs):
        if first:
            rhs, inverse, couple, own_rhs, y, keep, send, scaled, sums = refs
        else:
            y, couple, own_rhs, keep, send, scaled, sums = refs
        step = pl.program_id(0)

        @pl.when(step == 0)
        def _():
            for b in range(blocks):
                place = slice(b * block_rows, (b + 1) * block_rows)
                if first:
                    lower = lower_unit(inverse[b].astype(F32), 0).astype(BF16)
                    solved = nn(lower, rhs[b]).T.astype(BF16)
                    y[:, place] = solved
                else:
                    solved = y[:, place]
                scaled[:, place] = solved * mask[b, level - 1].astype(F32).astype(BF16)
            alone = (jnp.bitwise_and(info[LAYER], (1 << level) - 1) == 0).astype(F32)
            scaled[:, width:] = (own_rhs[0].astype(F32).T * -alone).astype(BF16)

        weights = jnp.concatenate([couple[b, 0] for b in range(blocks)], axis=1)
        row_ids = step * tile + lax.broadcasted_iota(jnp.int32, (tile, own_rows), 0)
        own_ids = info[ME] * own_rows + lax.broadcasted_iota(jnp.int32, (tile, own_rows), 1)
        chosen = (row_ids == own_ids).astype(F32).astype(BF16)
        total = nt(scaled[:, :width], weights) + nt(scaled[:, width:], chosen)
        sums[...] = total.astype(BF16)
        for slot in range(planes):
            rows = pl.ds(pl.multiple_of(info[SLOTS + slot] * cols, cols), cols)
            if slot < half:
                keep[slot] = sums[rows]
            else:
                send[slot - half] = sums[rows]

    def whole(shape):
        return pl.BlockSpec(shape, lambda t, info, mask: (0,) * len(shape))

    part = pl.BlockSpec((half, cols, tile), lambda t, info, mask: (0, 0, t))
    part_shape = jax.ShapeDtypeStruct((half, cols, sep_rows), BF16)
    y_shape = (rhs_cols, width)
    out = pl.pallas_call(
        kernel,
        grid_spec=pltpu.PrefetchScalarGridSpec(
            num_scalar_prefetch=2,
            grid=(sep_rows // tile,),
            in_specs=[whole(leaf.shape) for leaf in leaves]
            + [
                pl.BlockSpec((blocks, 1, tile, block_rows), lambda t, info, mask: (0, level - 1, t, 0)),
                pl.BlockSpec((1, own_rows, rhs_cols), lambda t, info, mask: (sep_id(info), 0, 0)),
            ],
            out_specs=([whole(y_shape)] if first else []) + [part, part],
            scratch_shapes=[
                pltpu.VMEM((rhs_cols, width + own_rows), BF16),
                pltpu.VMEM((rhs_cols, tile), BF16),
            ],
        ),
        out_shape=([jax.ShapeDtypeStruct(y_shape, BF16)] if first else []) + [part_shape, part_shape],
        compiler_params=VMEM,
        cost_estimate=pl.CostEstimate(
            flops=2 * rhs_cols * width * sep_rows, bytes_accessed=2 * width * sep_rows, transcendentals=0
        ),
        name="leaf_forward",
    )(info, mask, *leaves, couple, sep_rhs)
    return out


def paired(count):
    step = 2 if count % 2 == 0 else 1
    return [range(i, i + step) for i in range(0, count, step)]


def rows_times(pieces, part, vector, out, order):
    for group in paired(len(pieces)):
        rows = jnp.concatenate([pieces[i][part] for i in group], axis=0)
        result = nt(vector, rows)
        for at, i in enumerate(group):
            lanes = pl.ds(pl.multiple_of(order[i] * LANES, LANES), LANES)
            out[:, lanes] = result[:, at * LANES : (at + 1) * LANES].astype(out.dtype)


def times_rows(pieces, part, vector, order):
    total = None
    for group in paired(len(pieces)):
        rows = jnp.concatenate([pieces[i][part] for i in group], axis=0)
        left = jnp.concatenate(
            [vector[:, pl.ds(pl.multiple_of(order[i] * LANES, LANES), LANES)] for i in group], axis=1
        ).astype(BF16)
        term = nn(left, rows)
        total = term if total is None else total + term
    return total


def at_part(index):
    return slice(index * LANES, (index + 1) * LANES)


def vmem_call(kernel, order, arrays, out_shapes, scratch, name, flops):
    vmem = pl.BlockSpec(memory_space=pltpu.VMEM)
    return pl.pallas_call(
        kernel,
        in_specs=[pl.BlockSpec(memory_space=pltpu.SMEM)] + [vmem] * len(arrays),
        out_specs=[vmem] * len(out_shapes),
        out_shape=out_shapes,
        scratch_shapes=scratch,
        compiler_params=VMEM,
        cost_estimate=pl.CostEstimate(
            flops=flops, bytes_accessed=sum(a.size * a.dtype.itemsize for a in arrays), transcendentals=0
        ),
        name=name,
    )(order, *arrays)


def level_forward_call(order, ours, theirs, pieces, couples):
    count = len(pieces)

    def kernel(order, ours, theirs, *refs):
        pieces, outs = refs[:count], refs[count:]
        residual = (-(ours[...].astype(F32) + theirs[...].astype(F32))).astype(BF16)
        y = outs[0]
        rows_times(pieces, at_part(0), residual, y, order)
        for slot in range(couples):
            rows_times(pieces, at_part(slot + 1), y[...], outs[slot + 1], order)

    shapes = [jax.ShapeDtypeStruct(ours.shape, BF16)]
    shapes += [jax.ShapeDtypeStruct(ours.shape, F32)] * couples
    flops = 2 * ours.size * ours.shape[1] * (1 + couples)
    return vmem_call(kernel, order, [ours, theirs, *pieces], shapes, [], "level_forward", flops)


def top_call(order, ours, theirs, pieces, levels):
    count = len(pieces)

    def kernel(order, ours, theirs, *refs):
        pieces, (x, diag, y) = refs[:count], refs[count:]
        for i in range(count):
            lanes = pl.ds(pl.multiple_of(order[i] * LANES, LANES), LANES)
            split = pieces[i][LANES : LANES + DIAG_ROWS, :LANES].astype(F32)
            for level in range(levels):
                diag[level : level + 1, lanes] = split[2 * level : 2 * level + 1] + split[2 * level + 1 : 2 * level + 2]
        residual = (-(ours[...].astype(F32) + theirs[...].astype(F32))).astype(BF16)
        rows_times(pieces, at_part(0), residual, y, order)
        y[...] = y[...].astype(BF16).astype(F32) / diag[levels - 1 : levels]
        target = y[...].astype(BF16)
        y[...] = target.astype(F32)
        x[...] = times_rows(pieces, at_part(0), y, order).astype(BF16)

    shapes = [jax.ShapeDtypeStruct(ours.shape, BF16), jax.ShapeDtypeStruct((levels, ours.shape[1]), F32)]
    scratch = [pltpu.VMEM(ours.shape, F32)]
    flops = 4 * ours.size * ours.shape[1]
    return vmem_call(kernel, order, [ours, theirs, *pieces], shapes, scratch, "top_level", flops)


def level_backward_call(order, y, diag, uppers, pieces, level):
    count, above = len(pieces), len(uppers)

    def kernel(order, y, diag, *refs):
        uppers, pieces, (x, target) = refs[:above], refs[above : above + count], refs[above + count :]
        value = y[...].astype(F32) / diag[level - 1 : level]
        for slot in range(above):
            value = value - times_rows(pieces, at_part(slot + 1), uppers[slot], order)
        target[...] = value.astype(BF16)
        x[...] = times_rows(pieces, at_part(0), target, order).astype(BF16)

    shapes = [jax.ShapeDtypeStruct(y.shape, BF16)]
    scratch = [pltpu.VMEM(y.shape, BF16)]
    flops = 2 * y.size * y.shape[1] * (1 + above)
    return vmem_call(kernel, order, [y, diag, *uppers, *pieces], shapes, scratch, "level_backward", flops)[0]


def leaf_backward_call(info, mask, y, inverse, couple, diag, above, own_rows):
    blocks, levels, sep_rows, block_rows = couple.shape
    rhs_cols = y.shape[0]
    slots = len(above[0])
    cols = rhs_cols // slots
    pair = 2 if blocks % 2 == 0 else 1

    def kernel(info, mask, y, inverse, couple, diag, *refs):
        above = refs[: levels * slots]
        leaf_out, sep_out, whole, sems = refs[levels * slots :]
        step = pl.program_id(0)

        def fetch(level, slot):
            rows = pl.ds(pl.multiple_of(info[SLOTS + slot] * cols, cols), cols)
            return pltpu.make_async_copy(
                above[level * slots + slot], whole.at[level, rows], sems.at[level, slot]
            )

        @pl.when(step == 0)
        def _():
            for level in range(levels):
                for slot in range(slots):
                    fetch(level, slot).start()
            for level in range(levels):
                for slot in range(slots):
                    fetch(level, slot).wait()
            row_ids = info[ME] * own_rows + lax.broadcasted_iota(jnp.int32, (own_rows, sep_rows), 0)
            col_ids = lax.broadcasted_iota(jnp.int32, (own_rows, sep_rows), 1)
            chosen = (row_ids == col_ids).astype(F32).astype(BF16)
            for level in range(levels):
                sep_out[0, level] = nt(chosen, whole[level]).astype(BF16)

        terms = None
        for level in range(levels):
            weights = jnp.concatenate(
                [
                    couple[b, level] * mask[step * pair + b, level].astype(F32).astype(BF16)
                    for b in range(pair)
                ],
                axis=1,
            )
            term = nn(whole[level], weights)
            terms = term if terms is None else terms + term
        for b in range(pair):
            place = slice(b * block_rows, (b + 1) * block_rows)
            scale = 1.0 / diag[pl.ds(step * pair + b, 1)]
            target = (y[:, place].astype(F32) * scale - terms[:, place]).astype(BF16)
            lower = lower_unit(inverse[b].astype(F32), 0).T.astype(BF16)
            leaf_out[b] = nt(lower, target).astype(BF16)

    anywhere = pl.BlockSpec(memory_space=pl.ANY)
    return pl.pallas_call(
        kernel,
        grid_spec=pltpu.PrefetchScalarGridSpec(
            num_scalar_prefetch=2,
            grid=(blocks // pair,),
            in_specs=[
                pl.BlockSpec((rhs_cols, pair * block_rows), lambda t, info, mask: (0, t)),
                pl.BlockSpec((pair, block_rows, block_rows), lambda t, info, mask: (t, 0, 0)),
                pl.BlockSpec((pair, levels, sep_rows, block_rows), lambda t, info, mask: (t, 0, 0, 0)),
                pl.BlockSpec(diag.shape, lambda t, info, mask: (0, 0)),
            ]
            + [anywhere] * (levels * slots),
            out_specs=[
                pl.BlockSpec((pair, block_rows, rhs_cols), lambda t, info, mask: (t, 0, 0)),
                pl.BlockSpec((1, levels, own_rows, rhs_cols), lambda t, info, mask: (0, 0, 0, 0)),
            ],
            scratch_shapes=[
                pltpu.VMEM((levels, rhs_cols, sep_rows), BF16),
                pltpu.SemaphoreType.DMA((levels, slots)),
            ],
        ),
        out_shape=[
            jax.ShapeDtypeStruct((blocks, block_rows, rhs_cols), BF16),
            jax.ShapeDtypeStruct((1, levels, own_rows, rhs_cols), BF16),
        ],
        compiler_params=VMEM,
        cost_estimate=pl.CostEstimate(
            flops=2 * rhs_cols * blocks * block_rows * levels * sep_rows,
            bytes_accessed=2 * blocks * block_rows * levels * sep_rows,
            transcendentals=0,
        ),
        name="leaf_backward",
    )(info, mask, y, inverse, couple, diag, *[piece for level in above for piece in level])


def repacked(pieces, block_slot, parts, own_rows):
    planes, sep_rows = len(pieces), pieces[0].shape[-1]
    whole = jnp.concatenate(
        [lax.dynamic_index_in_dim(jnp.stack(pieces), block_slot[i], 0) for i in range(planes)], axis=0
    )
    count = planes * own_rows // LANES
    mats = whole[:, : parts * own_rows].reshape(count, planes // count, parts, own_rows, sep_rows)
    mats = jnp.transpose(mats, (0, 2, 1, 3, 4)).reshape(count, parts * LANES, sep_rows)
    rest = whole[:, parts * own_rows :, :own_rows]
    rest = rest.reshape(count, planes // count, rest.shape[1], own_rows)
    rest = jnp.transpose(rest, (0, 2, 1, 3)).reshape(count, rest.shape[2], LANES)
    rest = jnp.pad(rest, ((0, 0), (0, 0), (0, sep_rows - LANES)))
    mats = jnp.concatenate([mats, rest], axis=1)
    return [mats[i] for i in range(count)]


def body(
    leaf_rhs,
    leaf_inverse,
    leaf_couple,
    couple_mask,
    leaf_diag,
    sep_rhs,
    sep_inverse,
    sep_couple,
    sep_diag,
):
    levels = leaf_couple.shape[1]
    planes = lax.axis_size("plane")
    layers = lax.axis_size("layer")
    own_rows = sep_rhs.shape[1]
    layer_id = lax.axis_index("layer").astype(jnp.int32)
    me = lax.axis_index("plane").astype(jnp.int32)
    table = slot_table(planes)
    slot_block = lax.dynamic_index_in_dim(jnp.asarray(table), me, 0, keepdims=False)
    info = jnp.concatenate([jnp.stack([me, layer_id]), slot_block])

    groups = [
        gather(own) for own in collect_call(info, sep_inverse, sep_couple, sep_diag, levels, layers)
    ]
    order = slot_block
    if own_rows != LANES:
        inverse_table = np.argsort(table, axis=1).astype(np.int32)
        block_slot = lax.dynamic_index_in_dim(jnp.asarray(inverse_table), me, 0, keepdims=False)
        groups = [
            repacked(group, block_slot, 1 + levels - level, own_rows)
            for level, group in enumerate(groups, 1)
        ]
        order = jnp.arange(len(groups[0]), dtype=jnp.int32)

    sums = []
    leaf_y = None
    for level in range(1, levels + 1):
        leaves = [leaf_rhs, leaf_inverse] if level == 1 else [leaf_y]
        out = leaf_forward_call(info, couple_mask, leaves, leaf_couple, sep_rhs, level, layers)
        if level == 1:
            leaf_y = out[0]
        sums.append(scatter_sum(*out[-2:]))

    solved = []
    for level in range(1, levels + 1):
        theirs = [swap_layer(sums[upper], level - 1) for upper in range(level - 1, levels)]
        if level < levels:
            out = level_forward_call(order, sums[level - 1], theirs[0], groups[level - 1], levels - level)
            solved.append(out[0])
            for slot in range(levels - level):
                upper = level + slot
                sums[upper] = added(sums[upper], theirs[1 + slot], out[1 + slot])
    answers = [None] * levels
    answers[-1], diag = top_call(order, sums[-1], theirs[0], groups[-1], levels)
    for level in range(levels - 1, 0, -1):
        answers[level - 1] = level_backward_call(
            order, solved[level - 1], diag, answers[level:], groups[level - 1], level
        )
    above = [None] * levels
    for level in range(levels, 0, -1):
        above[level - 1] = gather(answers[level - 1])
    return tuple(
        leaf_backward_call(info, couple_mask, leaf_y, leaf_inverse, leaf_couple, leaf_diag, above, own_rows)
    )


def solution(mesh):
    in_specs = (
        P(("layer", "plane"), None, None),
        P(("layer", "plane"), None, None),
        P(("layer", "plane"), None, None, None),
        P(("layer", "plane"), None),
        P(("layer", "plane"), None),
        P(None, "plane", None),
        P(None, "plane", None),
        P(None, None, "plane", None),
        P(None, "plane"),
    )
    out_specs = (P(("layer", "plane"), None, None), P("layer", None, "plane", None))
    return jax.shard_map(body, mesh=mesh, in_specs=in_specs, out_specs=out_specs, check_vma=False)
```

```python
import jax
import jax.numpy as jnp
from jax import lax
from jax.experimental import pallas as pl
from jax.experimental.pallas import tpu as pltpu
from jax.sharding import PartitionSpec as P

F32 = jnp.float32
BF16 = jnp.bfloat16
LANES = 128
TILE = 256
DIAG_ROWS = 16
NT = (((1,), (1,)), ((), ()))
VMEM = pltpu.CompilerParams(vmem_limit_bytes=32 * 1024 * 1024)


def bit_orders(planes):
    link_bits = list(range(1, planes.bit_length() - 1))
    turn = len(link_bits) // 2
    return [link_bits, link_bits[turn:] + link_bits[:turn]]


def slot_table(planes, parity):
    orders = bit_orders(planes)
    count = len(orders[0])
    table = []
    for slot in range(planes):
        other = slot >> count
        block = other
        for place, bit in enumerate(orders[parity ^ other]):
            if slot >> (count - 1 - place) & 1:
                block ^= 1 << bit
        table.append(block)
    return table


def swap_core(value):
    planes = lax.axis_size("plane")
    return lax.ppermute(value, "plane", [(i, i ^ 1) for i in range(planes)])


def swap_link(value, place):
    planes, layers = lax.axis_size("plane"), lax.axis_size("layer")
    orders = bit_orders(planes)
    pairs = []
    for layer in range(layers):
        for i in range(planes):
            bit = orders[(i ^ layer) & 1][place]
            pairs.append((layer * planes + i, layer * planes + (i ^ (1 << bit))))
    return lax.ppermute(value, ("layer", "plane"), pairs)


def swap_layer(value, stride):
    layers = lax.axis_size("layer")
    return lax.ppermute(value, "layer", [(i, i ^ (1 << stride)) for i in range(layers)])


def after(value, *others):
    return lax.optimization_barrier((value, *others))[0]


def after_all(values, *others):
    return lax.optimization_barrier((*values, *others))[: len(values)]


def added(*terms):
    total = terms[0].astype(F32)
    for term in terms[1:]:
        total = total + term.astype(F32)
    return total.astype(BF16)


def scatter_sum(low, high, first_after):
    arrived = []
    for place in range(len(bit_orders(lax.axis_size("plane"))[0])):
        send = added(*high)
        if place == 0:
            send = after(send, *first_after)
        arrived.append(swap_link(send, place))
        terms = [*low, arrived[-1]]
        half = terms[0].shape[0] // 2
        low, high = [term[:half] for term in terms], [term[half:] for term in terms]
    return added(*[term[0] for term in terms]), arrived


def gather(value, cross=True):
    pieces = [value]
    for place in reversed(range(len(bit_orders(lax.axis_size("plane"))[0]))):
        pieces = pieces + [swap_link(piece, place) for piece in pieces]
    return pieces + [swap_core(piece) for piece in pieces] if cross else pieces


def lower_unit(block, first_row):
    row_count = block.shape[-2]
    col_count = block.shape[-1]
    row_ids = first_row + lax.broadcasted_iota(jnp.int32, (row_count, col_count), 0)
    col_ids = lax.broadcasted_iota(jnp.int32, (row_count, col_count), 1)
    below = jnp.where(col_ids < row_ids, block, jnp.zeros_like(block))
    return jnp.where(col_ids == row_ids, jnp.ones_like(block), below)


def nt(left, right):
    return lax.dot_general(left, right, NT, preferred_element_type=F32)


def nn(left, right):
    return jnp.dot(left, right, preferred_element_type=F32)


def places():
    return lax.axis_index("plane").astype(jnp.int32), lax.axis_index("layer").astype(jnp.int32)


def slot_blocks(planes):
    me, layer_id = places()
    parity = jnp.bitwise_and(jnp.bitwise_xor(me, layer_id), 1)
    even, odd = slot_table(planes, 0), slot_table(planes, 1)
    return [jnp.bitwise_xor(me, even[i] + parity * (odd[i] - even[i])) for i in range(planes)]


def at_multiple(index, size):
    return pl.ds(pl.multiple_of(index * size, size), size)


def sep_index(layer_id, level, layers):
    return layers - (layers >> level - 1) + jnp.right_shift(layer_id, level)


def kernel_call(kernel, arrays, spaces, out_shapes, scratch, name, flops=1, out_space=pltpu.VMEM, aliases={}):
    arrays = [
        pltpu.with_memory_space_constraint(array, space) if space == pltpu.HBM else array
        for array, space in zip(arrays, spaces)
    ]
    return pl.pallas_call(
        kernel,
        in_specs=[pl.BlockSpec(memory_space=space) for space in spaces],
        out_specs=[pl.BlockSpec(memory_space=out_space)] * len(out_shapes),
        out_shape=out_shapes,
        scratch_shapes=scratch,
        input_output_aliases=aliases,
        compiler_params=VMEM,
        cost_estimate=pl.CostEstimate(flops=flops, bytes_accessed=1, transcendentals=0),
        name=name,
    )(*arrays)


def collect_call(sep_inverse, sep_couple, sep_diag, levels, layers):
    own_rows, sep_rows = sep_inverse.shape[1:]

    def kernel(inverse, couple, diag_in, *refs):
        outs, (held, diag, sems, couple_sems) = refs[:levels], refs[levels:]
        me, layer_id = places()
        diag_load = pltpu.make_async_copy(diag_in, diag, sems.at[levels])
        diag_load.start()
        loads, moves = [], []
        for level in range(1, levels + 1):
            sep = sep_index(layer_id, level, layers)
            loads.append(pltpu.make_async_copy(inverse.at[sep], held.at[level - 1], sems.at[level - 1]))
            loads[-1].start()
            for slot in range(levels - level):
                rows = slice((slot + 1) * own_rows, (slot + 2) * own_rows)
                moves.append(
                    pltpu.make_async_copy(
                        couple.at[sep, slot], outs[level - 1].at[rows], couple_sems.at[level - 1, slot]
                    )
                )
                moves[-1].start()
        diag_load.wait()
        rows = []
        for level in range(1, levels + 1):
            value = diag[pl.ds(sep_index(layer_id, level, layers), 1)]
            high = value.astype(BF16).astype(F32)
            rows += [high, value - high]
        rows.append(jnp.zeros((DIAG_ROWS - len(rows), own_rows), F32))
        below = levels * own_rows
        outs[0][below:] = jnp.zeros((DIAG_ROWS, sep_rows), BF16)
        outs[0][below:, :own_rows] = jnp.concatenate(rows, axis=0).astype(BF16)
        for level in range(1, levels + 1):
            loads[level - 1].wait()
            lower = lower_unit(held[level - 1].astype(F32), me * own_rows)
            outs[level - 1][:own_rows] = lower.astype(BF16)
        for move in moves:
            move.wait()

    shapes = [((1 + levels - level) * own_rows, sep_rows) for level in range(1, levels + 1)]
    shapes[0] = (levels * own_rows + DIAG_ROWS, sep_rows)
    return kernel_call(
        kernel,
        [sep_inverse, sep_couple, sep_diag],
        [pltpu.HBM] * 3,
        [jax.ShapeDtypeStruct(shape, BF16) for shape in shapes],
        [
            pltpu.VMEM((levels, own_rows, sep_rows), BF16),
            pltpu.VMEM(sep_diag.shape, F32),
            pltpu.SemaphoreType.DMA((levels + 1,)),
            pltpu.SemaphoreType.DMA((levels, levels)),
        ],
        "collect",
        flops=20_000_000_000,
    )


def leaf_forward_call(mask, leaves, couple, sep_rhs, slots, layers):
    first = len(leaves) == 2
    blocks, levels, sep_rows, block_rows = couple.shape
    own_rows, rhs_cols = sep_rhs.shape[1:]
    planes = sep_rows // own_rows
    cols = rhs_cols // planes
    here = len(slots) * cols
    width = blocks * block_rows
    tile = min(TILE, sep_rows)
    tiles = sep_rows // tile

    def kernel(mask, *refs):
        if first:
            rhs, inverse, couple, own_rhs, y, *parts, scaled, turned = refs
        else:
            y, couple, own_rhs, *parts, scaled, turned = refs
        me, layer_id = places()
        order = slot_blocks(planes)
        if first:
            for b in range(blocks):
                lower = lower_unit(inverse[b].astype(F32), 0).astype(BF16)
                y[:, b * block_rows : (b + 1) * block_rows] = nn(lower, rhs[b]).T.astype(BF16)
        for level in range(levels):
            alone = (jnp.bitwise_and(layer_id, (2 << level) - 1) == 0).astype(F32)
            own = own_rhs[sep_index(layer_id, level + 1, layers)].astype(F32)
            turned[...] = (own.T * -alone).astype(BF16)
            for at, slot in enumerate(slots):
                rows = slice(at * cols, (at + 1) * cols)
                scaled[level, rows, width:] = turned[at_multiple(order[slot], cols)]
                for b in range(blocks):
                    place = slice(b * block_rows, (b + 1) * block_rows)
                    used = mask[level : level + 1, b : b + 1].astype(F32).astype(BF16)
                    scaled[level, rows, place] = y[at_multiple(order[slot], cols), place] * used
        for level in range(levels):
            for t in range(tiles):
                lanes = slice(t * tile, (t + 1) * tile)
                row_ids = t * tile + lax.broadcasted_iota(jnp.int32, (tile, own_rows), 0)
                own_ids = me * own_rows + lax.broadcasted_iota(jnp.int32, (tile, own_rows), 1)
                chosen = (row_ids == own_ids).astype(F32).astype(BF16)
                weights = jnp.concatenate([couple[b, level, lanes] for b in range(blocks)] + [chosen], axis=1)
                total = nt(scaled[level], weights).astype(BF16)
                half = len(slots) // 2
                for at in range(len(slots)):
                    parts[at // half][at % half, level, :, lanes] = total[at * cols : (at + 1) * cols]

    part = jax.ShapeDtypeStruct((len(slots) // 2, levels, cols, sep_rows), BF16)
    y_shape = [jax.ShapeDtypeStruct((rhs_cols, width), BF16)] if first else []
    scratch = [pltpu.VMEM((levels, here, width + own_rows), BF16), pltpu.VMEM((rhs_cols, own_rows), BF16)]
    arrays = [mask, *leaves, couple, sep_rhs]
    return vmem_call(kernel, arrays, y_shape + [part] * 2, scratch, "leaf_forward")


def paired(count):
    step = 2 if count % 2 == 0 else 1
    return [range(i, i + step) for i in range(0, count, step)]


def rows_times(pieces, part, vector, out, order):
    for group in paired(len(pieces)):
        rows = jnp.concatenate([pieces[i][part] for i in group], axis=0)
        result = nt(vector, rows)
        for at, i in enumerate(group):
            lanes = pl.ds(pl.multiple_of(order[i] * LANES, LANES), LANES)
            out[:, lanes] = result[:, at * LANES : (at + 1) * LANES].astype(out.dtype)


def times_rows(pieces, part, vector, order):
    total = None
    for group in paired(len(pieces)):
        rows = jnp.concatenate([pieces[i][part] for i in group], axis=0)
        left = jnp.concatenate(
            [vector[:, pl.ds(pl.multiple_of(order[i] * LANES, LANES), LANES)] for i in group], axis=1
        ).astype(BF16)
        term = nn(left, rows)
        total = term if total is None else total + term
    return total


def at_part(index):
    return slice(index * LANES, (index + 1) * LANES)


def vmem_call(kernel, arrays, out_shapes, scratch, name):
    return kernel_call(kernel, arrays, [pltpu.VMEM] * len(arrays), out_shapes, scratch, name)


def piece_order(count, planes):
    return slot_blocks(planes) if count == planes else list(range(count))


def level_forward_call(planes, sums, pieces):
    count = len(pieces)
    levels = sums.shape[0]

    def kernel(sums, *refs):
        order = piece_order(count, planes)
        pieces, (y, outs, work) = refs[:count], refs[count:]
        rows_times(pieces, at_part(0), -sums[0], y, order)
        for level in range(1, levels):
            rows_times(pieces, at_part(level), y[...], work, order)
            outs[level - 1] = (sums[level].astype(F32) + work[...]).astype(BF16)

    shape = sums.shape[1:]
    shapes = [jax.ShapeDtypeStruct(shape, BF16), jax.ShapeDtypeStruct((levels - 1, *shape), BF16)]
    return vmem_call(kernel, [sums, *pieces], shapes, [pltpu.VMEM(shape, F32)], "level_forward")


def backward_call(planes, sums, solved, groups):
    levels = len(groups)
    count = len(groups[0])
    lower = levels - 1

    def kernel(sums, *refs):
        order = piece_order(count, planes)
        solved, refs = refs[:lower], refs[lower:]
        pieces, (out, diag, work) = [refs[i * count : (i + 1) * count] for i in range(levels)], refs[-3:]
        for i in range(count):
            split = pieces[0][i][levels * LANES : levels * LANES + DIAG_ROWS, :LANES].astype(F32)
            for level in range(levels):
                value = split[2 * level : 2 * level + 1] + split[2 * level + 1 : 2 * level + 2]
                diag[level : level + 1, at_multiple(order[i], LANES)] = value
        rows_times(pieces[-1], at_part(0), -sums[0], work, order)
        for level in range(levels, 0, -1):
            y = work if level == levels else solved[level - 1]
            value = y[...].astype(F32) / diag[level - 1 : level]
            for slot in range(levels - level):
                upper = out.at[level + slot]
                value = value - times_rows(pieces[level - 1], at_part(slot + 1), upper, order)
            work[...] = value.astype(BF16)
            out[level - 1] = times_rows(pieces[level - 1], at_part(0), work, order).astype(BF16)

    arrays = [sums, *solved, *[piece for group in groups for piece in group]]
    shape = sums.shape[1:]
    shapes = [jax.ShapeDtypeStruct((levels, *shape), BF16)]
    scratch = [pltpu.VMEM((levels, shape[1]), F32), pltpu.VMEM(shape, BF16)]
    return vmem_call(kernel, arrays, shapes, scratch, "backward")[0]


def leaf_backward_call(mask, y, inverse, couple, diag, above, groups, before, own_rows):
    blocks, levels, sep_rows, block_rows = couple.shape
    rhs_cols, width = y.shape
    planes = sep_rows // own_rows
    cols = rhs_cols // planes
    slots = [slot for group in groups for slot in group]
    size = len(groups[0]) * cols
    here = len(slots) * cols
    pair = 2 if blocks % 2 == 0 else 1
    steps = blocks // pair
    kept = len(before)

    def kernel(mask, y, inverse, couple, diag, *refs):
        pieces, refs = dict(zip(slots, refs)), refs[len(slots) + kept :]
        leaf_to, sep_to, whole, ys, leaf_out, sep_out, sems = refs
        me = places()[0]
        order = slot_blocks(planes)
        stores = []

        def store(source, target):
            stores.append(pltpu.make_async_copy(source, target, sems.at[len(stores)]))
            stores[-1].start()

        lanes = []
        for j, group in enumerate(groups):
            lanes.append(at_multiple(order[group[0]] // len(group), size))
            rows = slice(j * size, (j + 1) * size)
            ys[rows] = y[lanes[j]]
            for slot in group:
                row = j * size + lax.rem(order[slot], len(group)) * cols
                for level in range(levels):
                    whole[level, pl.ds(pl.multiple_of(row, cols), cols)] = pieces[slot][level]
        row_ids = me * own_rows + lax.broadcasted_iota(jnp.int32, (own_rows, sep_rows), 0)
        col_ids = lax.broadcasted_iota(jnp.int32, (own_rows, sep_rows), 1)
        chosen = (row_ids == col_ids).astype(F32).astype(BF16)
        for level in range(levels):
            sep_out[level] = nt(chosen, whole[level]).astype(BF16)
            for j in range(len(groups)):
                store(sep_out.at[level, :, j * size : (j + 1) * size], sep_to.at[0, level, :, lanes[j]])
        for step in range(steps):
            terms = [None] * pair
            for level in range(levels):
                weights = jnp.concatenate([couple[step * pair + b, level] for b in range(pair)], axis=1)
                value = nn(whole[level], weights)
                for b in range(pair):
                    place = slice(b * block_rows, (b + 1) * block_rows)
                    at = step * pair + b
                    term = value[:, place] * mask[level : level + 1, at : at + 1].astype(F32)
                    terms[b] = term if terms[b] is None else terms[b] + term
            for b in range(pair):
                at = step * pair + b
                place = slice(at * block_rows, (at + 1) * block_rows)
                scale = 1.0 / diag[at : at + 1]
                target = (ys[:, place].astype(F32) * scale - terms[b]).astype(BF16)
                lower = lower_unit(inverse[at].astype(F32), 0).T.astype(BF16)
                leaf_out[at] = nt(lower, target).astype(BF16)
            at = slice(step * pair, (step + 1) * pair)
            for j in range(len(groups)):
                store(leaf_out.at[at, :, j * size : (j + 1) * size], leaf_to.at[at, :, lanes[j]])
        for copy in stores:
            copy.wait()

    arrays = [mask, y, inverse, couple, diag, *[above[slot] for slot in slots], *before]
    shapes = [
        jax.ShapeDtypeStruct((blocks, block_rows, rhs_cols), BF16),
        jax.ShapeDtypeStruct((1, levels, own_rows, rhs_cols), BF16),
    ]
    scratch = [
        pltpu.VMEM((levels, here, sep_rows), BF16),
        pltpu.VMEM((here, width), BF16),
        pltpu.VMEM((blocks, block_rows, here), BF16),
        pltpu.VMEM((levels, own_rows, here), BF16),
        pltpu.SemaphoreType.DMA(((levels + steps) * len(groups),)),
    ]
    spaces = [pltpu.VMEM] * (len(arrays) - kept) + [pl.ANY] * kept
    aliases = {len(arrays) - kept + i: i for i in range(kept)}
    return kernel_call(
        kernel, arrays, spaces, shapes, scratch, "leaf_backward", out_space=pl.ANY, aliases=aliases
    )


def repacked(pieces, block_slot, parts, own_rows):
    planes, sep_rows = len(pieces), pieces[0].shape[-1]
    whole = jnp.concatenate(
        [lax.dynamic_index_in_dim(jnp.stack(pieces), block_slot[i], 0) for i in range(planes)], axis=0
    )
    count = planes * own_rows // LANES
    mats = whole[:, : parts * own_rows].reshape(count, planes // count, parts, own_rows, sep_rows)
    mats = jnp.transpose(mats, (0, 2, 1, 3, 4)).reshape(count, parts * LANES, sep_rows)
    rest = whole[:, parts * own_rows :, :own_rows]
    rest = rest.reshape(count, planes // count, rest.shape[1], own_rows)
    rest = jnp.transpose(rest, (0, 2, 1, 3)).reshape(count, rest.shape[2], LANES)
    rest = jnp.pad(rest, ((0, 0), (0, 0), (0, sep_rows - LANES)))
    mats = jnp.concatenate([mats, rest], axis=1)
    return [mats[i] for i in range(count)]


def body(
    leaf_rhs,
    leaf_inverse,
    leaf_couple,
    couple_mask,
    leaf_diag,
    sep_rhs,
    sep_inverse,
    sep_couple,
    sep_diag,
):
    levels = leaf_couple.shape[1]
    planes = lax.axis_size("plane")
    layers = lax.axis_size("layer")
    own_rows = sep_rhs.shape[1]

    own = collect_call(sep_inverse, sep_couple, sep_diag, levels, layers)
    mask = after(couple_mask.T, own[0])

    links = len(bit_orders(planes)[0])
    four = links == 2
    near = swap_link(own[0], links - 1) if four else own[0]
    quarter = planes // 4
    highs = [slot for slot in range(planes) if slot // quarter % 2 == 1]
    lows = [slot for slot in range(planes) if slot // quarter % 2 == 0]
    leaf_y, keep, send = leaf_forward_call(
        mask, [leaf_rhs, leaf_inverse], leaf_couple, sep_rhs, highs, layers
    )
    high = [after(keep, near), swap_core(send)]
    keep, send = leaf_forward_call(mask, [leaf_y], leaf_couple, sep_rhs, lows, layers)
    own_crossed = [swap_core(own[0]), swap_core(own[-1])] if four else []
    low = [after(keep, *own_crossed), swap_core(send)]
    sums, arrived = scatter_sum(low, high, [])

    def fitted(pieces, level):
        if own_rows == LANES:
            return pieces
        me = lax.axis_index("plane")
        parity = jnp.bitwise_and(jnp.bitwise_xor(me, lax.axis_index("layer")), 1)
        slots = jnp.bitwise_xor(me, jnp.asarray([slot_table(planes, 0), slot_table(planes, 1)])[parity])
        return repacked(pieces, jnp.argsort(slots).astype(jnp.int32), 1 + levels - level, own_rows)

    if four:
        near_crossed = swap_core(after(near, keep))
        side = swap_layer(near, 0)
        far = swap_link(after(near, arrived[0]), 0)
        last_own = after(own[-1], arrived[0])
        last_near = swap_link(last_own, 1)
        sums = after(sums, near_crossed, side)
        last = [own[-1], last_near, swap_link(after(last_own, arrived[1]), 0)]
    else:
        first = gather(own[0])
    groups, solved = [], []
    for level in range(1, levels + 1):
        sums = added(sums, swap_layer(sums, level - 1))
        if level == 1:
            if four:
                side, far = after_all([side, far], sums, last_near)
                first = [own[0], near, side, far, own_crossed[0], near_crossed, swap_core(side), swap_core(far)]
            groups.append(fitted(first, 1))
        elif four and level == levels:
            groups.append(fitted(last + [swap_core(piece) for piece in last[2:4]], level))
        else:
            groups.append(fitted(gather(own[level - 1]), level))
        if level < levels:
            y, sums = level_forward_call(planes, sums, groups[level - 1])
            solved.append(y)
        if level == 1 and four:
            last = last + [swap_link(last_near, 0), own_crossed[1], swap_core(after(last_near, y))]
    answers = backward_call(planes, sums, solved, groups)
    leaves = [mask, leaf_y, leaf_inverse, leaf_couple, leaf_diag]
    if not four or 2 * answers.shape[1] != LANES:
        above = dict(enumerate(gather(answers)))
        return tuple(leaf_backward_call(*leaves, above, [list(range(planes))], [], own_rows))
    above = dict(enumerate(gather(answers, cross=False)))
    for slot in range(3):
        above[4 + slot] = swap_core(above[slot])
    early = leaf_backward_call(*leaves, above, [[0, 4], [1, 6], [2, 5]], [], own_rows)
    above[7] = swap_core(after(above[3], early[0]))
    return tuple(leaf_backward_call(*leaves, above, [[3, 7]], early, own_rows))


def solution(mesh):
    in_specs = (
        P(("layer", "plane"), None, None),
        P(("layer", "plane"), None, None),
        P(("layer", "plane"), None, None, None),
        P(("layer", "plane"), None),
        P(("layer", "plane"), None),
        P(None, "plane", None),
        P(None, "plane", None),
        P(None, None, "plane", None),
        P(None, "plane"),
    )
    out_specs = (P(("layer", "plane"), None, None), P("layer", None, "plane", None))
    return jax.shard_map(body, mesh=mesh, in_specs=in_specs, out_specs=out_specs, check_vma=False)
```

```python
import jax
import jax.numpy as jnp
from jax import lax
from jax.experimental import pallas as pl
from jax.experimental.pallas import tpu as pltpu
from jax.sharding import PartitionSpec as P

F32 = jnp.float32
BF16 = jnp.bfloat16
LANES = 128
TILE = 256
DIAG_ROWS = 16
NT = (((1,), (1,)), ((), ()))
VMEM = pltpu.CompilerParams(vmem_limit_bytes=32 * 1024 * 1024)


def bit_orders(planes):
    link_bits = list(range(1, planes.bit_length() - 1))
    turn = len(link_bits) // 2
    return [link_bits, link_bits[turn:] + link_bits[:turn]]


def slot_table(planes, parity):
    orders = bit_orders(planes)
    count = len(orders[0])
    table = []
    for slot in range(planes):
        other = slot >> count
        block = other
        for place, bit in enumerate(orders[parity ^ other]):
            if slot >> (count - 1 - place) & 1:
                block ^= 1 << bit
        table.append(block)
    return table


def swap_core(value):
    planes = lax.axis_size("plane")
    return lax.ppermute(value, "plane", [(i, i ^ 1) for i in range(planes)])


def swap_link(value, place):
    planes, layers = lax.axis_size("plane"), lax.axis_size("layer")
    orders = bit_orders(planes)
    pairs = []
    for layer in range(layers):
        for i in range(planes):
            bit = orders[(i ^ layer) & 1][place]
            pairs.append((layer * planes + i, layer * planes + (i ^ (1 << bit))))
    return lax.ppermute(value, ("layer", "plane"), pairs)


def swap_layer(value, stride):
    layers = lax.axis_size("layer")
    return lax.ppermute(value, "layer", [(i, i ^ (1 << stride)) for i in range(layers)])


def after(value, *others):
    return lax.optimization_barrier((value, *others))[0]


def after_all(values, *others):
    return lax.optimization_barrier((*values, *others))[: len(values)]


def added(*terms):
    total = terms[0].astype(F32)
    for term in terms[1:]:
        total = total + term.astype(F32)
    return total.astype(BF16)


def scatter_sum(low, high, first_after):
    arrived = []
    for place in range(len(bit_orders(lax.axis_size("plane"))[0])):
        send = added(*high)
        if place == 0:
            send = after(send, *first_after)
        arrived.append(swap_link(send, place))
        terms = [*low, arrived[-1]]
        half = terms[0].shape[0] // 2
        low, high = [term[:half] for term in terms], [term[half:] for term in terms]
    return added(*[term[0] for term in terms]), arrived


def gather(value, cross=True):
    pieces = [value]
    for place in reversed(range(len(bit_orders(lax.axis_size("plane"))[0]))):
        pieces = pieces + [swap_link(piece, place) for piece in pieces]
    return pieces + [swap_core(piece) for piece in pieces] if cross else pieces


def lower_unit(block, first_row):
    row_count = block.shape[-2]
    col_count = block.shape[-1]
    row_ids = first_row + lax.broadcasted_iota(jnp.int32, (row_count, col_count), 0)
    col_ids = lax.broadcasted_iota(jnp.int32, (row_count, col_count), 1)
    below = jnp.where(col_ids < row_ids, block, jnp.zeros_like(block))
    return jnp.where(col_ids == row_ids, jnp.ones_like(block), below)


def nt(left, right):
    return lax.dot_general(left, right, NT, preferred_element_type=F32)


def nn(left, right):
    return jnp.dot(left, right, preferred_element_type=F32)


def places():
    return lax.axis_index("plane").astype(jnp.int32), lax.axis_index("layer").astype(jnp.int32)


def slot_blocks(planes):
    me, layer_id = places()
    parity = jnp.bitwise_and(jnp.bitwise_xor(me, layer_id), 1)
    even, odd = slot_table(planes, 0), slot_table(planes, 1)
    return [jnp.bitwise_xor(me, even[i] + parity * (odd[i] - even[i])) for i in range(planes)]


def at_multiple(index, size):
    return pl.ds(pl.multiple_of(index * size, size), size)


def sep_index(layer_id, level, layers):
    return layers - (layers >> level - 1) + jnp.right_shift(layer_id, level)


def kernel_call(kernel, arrays, spaces, out_shapes, scratch, name, flops=1, out_space=pltpu.VMEM, aliases={}):
    arrays = [
        pltpu.with_memory_space_constraint(array, space) if space == pltpu.HBM else array
        for array, space in zip(arrays, spaces)
    ]
    return pl.pallas_call(
        kernel,
        in_specs=[pl.BlockSpec(memory_space=space) for space in spaces],
        out_specs=[pl.BlockSpec(memory_space=out_space)] * len(out_shapes),
        out_shape=out_shapes,
        scratch_shapes=scratch,
        input_output_aliases=aliases,
        compiler_params=VMEM,
        cost_estimate=pl.CostEstimate(flops=flops, bytes_accessed=1, transcendentals=0),
        name=name,
    )(*arrays)


def collect_call(sep_inverse, sep_couple, sep_diag, levels, layers):
    own_rows, sep_rows = sep_inverse.shape[1:]

    def kernel(inverse, couple, diag_in, *refs):
        outs, (held, diag, sems, couple_sems) = refs[:levels], refs[levels:]
        me, layer_id = places()
        diag_load = pltpu.make_async_copy(diag_in, diag, sems.at[levels])
        diag_load.start()
        loads, moves = [], []
        for level in range(1, levels + 1):
            sep = sep_index(layer_id, level, layers)
            loads.append(pltpu.make_async_copy(inverse.at[sep], held.at[level - 1], sems.at[level - 1]))
            loads[-1].start()
            for slot in range(levels - level):
                rows = slice((slot + 1) * own_rows, (slot + 2) * own_rows)
                moves.append(
                    pltpu.make_async_copy(
                        couple.at[sep, slot], outs[level - 1].at[rows], couple_sems.at[level - 1, slot]
                    )
                )
                moves[-1].start()
        diag_load.wait()
        rows = []
        for level in range(1, levels + 1):
            value = diag[pl.ds(sep_index(layer_id, level, layers), 1)]
            high = value.astype(BF16).astype(F32)
            rows += [high, value - high]
        rows.append(jnp.zeros((DIAG_ROWS - len(rows), own_rows), F32))
        below = levels * own_rows
        outs[0][below:] = jnp.zeros((DIAG_ROWS, sep_rows), BF16)
        outs[0][below:, :own_rows] = jnp.concatenate(rows, axis=0).astype(BF16)
        for level in range(1, levels + 1):
            loads[level - 1].wait()
            lower = lower_unit(held[level - 1].astype(F32), me * own_rows)
            outs[level - 1][:own_rows] = lower.astype(BF16)
        for move in moves:
            move.wait()

    shapes = [((1 + levels - level) * own_rows, sep_rows) for level in range(1, levels + 1)]
    shapes[0] = (levels * own_rows + DIAG_ROWS, sep_rows)
    return kernel_call(
        kernel,
        [sep_inverse, sep_couple, sep_diag],
        [pltpu.HBM] * 3,
        [jax.ShapeDtypeStruct(shape, BF16) for shape in shapes],
        [
            pltpu.VMEM((levels, own_rows, sep_rows), BF16),
            pltpu.VMEM(sep_diag.shape, F32),
            pltpu.SemaphoreType.DMA((levels + 1,)),
            pltpu.SemaphoreType.DMA((levels, levels)),
        ],
        "collect",
        flops=20_000_000_000,
    )


def leaf_forward_call(mask, leaves, couple, sep_rhs, slots, layers):
    first = len(leaves) == 2
    blocks, levels, sep_rows, block_rows = couple.shape
    own_rows, rhs_cols = sep_rhs.shape[1:]
    planes = sep_rows // own_rows
    cols = rhs_cols // planes
    here = len(slots) * cols
    width = blocks * block_rows
    tile = min(TILE, sep_rows)
    tiles = sep_rows // tile

    def kernel(mask, *refs):
        if first:
            rhs, inverse, couple, own_rhs, y, *parts, scaled, turned = refs
        else:
            y, couple, own_rhs, *parts, scaled, turned = refs
        me, layer_id = places()
        order = slot_blocks(planes)
        if first:
            for b in range(blocks):
                lower = lower_unit(inverse[b].astype(F32), 0).astype(BF16)
                y[:, b * block_rows : (b + 1) * block_rows] = nn(lower, rhs[b]).T.astype(BF16)
        for level in range(levels):
            alone = (jnp.bitwise_and(layer_id, (2 << level) - 1) == 0).astype(F32)
            own = own_rhs[sep_index(layer_id, level + 1, layers)].astype(F32)
            turned[...] = (own.T * -alone).astype(BF16)
            for at, slot in enumerate(slots):
                rows = slice(at * cols, (at + 1) * cols)
                scaled[level, rows, width:] = turned[at_multiple(order[slot], cols)]
                for b in range(blocks):
                    place = slice(b * block_rows, (b + 1) * block_rows)
                    used = mask[level : level + 1, b : b + 1].astype(F32).astype(BF16)
                    scaled[level, rows, place] = y[at_multiple(order[slot], cols), place] * used
        for level in range(levels):
            for t in range(tiles):
                lanes = slice(t * tile, (t + 1) * tile)
                row_ids = t * tile + lax.broadcasted_iota(jnp.int32, (tile, own_rows), 0)
                own_ids = me * own_rows + lax.broadcasted_iota(jnp.int32, (tile, own_rows), 1)
                chosen = (row_ids == own_ids).astype(F32).astype(BF16)
                weights = jnp.concatenate([couple[b, level, lanes] for b in range(blocks)] + [chosen], axis=1)
                total = nt(scaled[level], weights).astype(BF16)
                half = len(slots) // 2
                for at in range(len(slots)):
                    parts[at // half][at % half, level, :, lanes] = total[at * cols : (at + 1) * cols]

    part = jax.ShapeDtypeStruct((len(slots) // 2, levels, cols, sep_rows), BF16)
    y_shape = [jax.ShapeDtypeStruct((rhs_cols, width), BF16)] if first else []
    scratch = [pltpu.VMEM((levels, here, width + own_rows), BF16), pltpu.VMEM((rhs_cols, own_rows), BF16)]
    arrays = [mask, *leaves, couple, sep_rhs]
    return vmem_call(kernel, arrays, y_shape + [part] * 2, scratch, "leaf_forward")


def added_call(ours, theirs, flops):
    def kernel(ours, theirs, out):
        out[...] = (ours[...].astype(F32) + theirs[...].astype(F32)).astype(BF16)

    spaces = [pltpu.VMEM] * 2
    shapes = [jax.ShapeDtypeStruct(ours.shape, BF16)]
    return kernel_call(kernel, [ours, theirs], spaces, shapes, [], "added", flops)[0]


def paired(count):
    step = 2 if count % 2 == 0 else 1
    return [range(i, i + step) for i in range(0, count, step)]


def rows_times(pieces, part, vector, out, order):
    for group in paired(len(pieces)):
        rows = jnp.concatenate([pieces[i][part] for i in group], axis=0)
        result = nt(vector, rows)
        for at, i in enumerate(group):
            lanes = pl.ds(pl.multiple_of(order[i] * LANES, LANES), LANES)
            out[:, lanes] = result[:, at * LANES : (at + 1) * LANES].astype(out.dtype)


def times_rows(pieces, part, vector, order):
    total = None
    for group in paired(len(pieces)):
        rows = jnp.concatenate([pieces[i][part] for i in group], axis=0)
        left = jnp.concatenate(
            [vector[:, pl.ds(pl.multiple_of(order[i] * LANES, LANES), LANES)] for i in group], axis=1
        ).astype(BF16)
        term = nn(left, rows)
        total = term if total is None else total + term
    return total


def at_part(index):
    return slice(index * LANES, (index + 1) * LANES)


def vmem_call(kernel, arrays, out_shapes, scratch, name):
    return kernel_call(kernel, arrays, [pltpu.VMEM] * len(arrays), out_shapes, scratch, name)


def piece_order(count, planes):
    return slot_blocks(planes) if count == planes else list(range(count))


def level_forward_call(planes, sums, pieces):
    count = len(pieces)
    levels = sums.shape[0]

    def kernel(sums, *refs):
        order = piece_order(count, planes)
        pieces, (y, outs, work) = refs[:count], refs[count:]
        rows_times(pieces, at_part(0), -sums[0], y, order)
        for level in range(1, levels):
            rows_times(pieces, at_part(level), y[...], work, order)
            outs[level - 1] = (sums[level].astype(F32) + work[...]).astype(BF16)

    shape = sums.shape[1:]
    shapes = [jax.ShapeDtypeStruct(shape, BF16), jax.ShapeDtypeStruct((levels - 1, *shape), BF16)]
    return vmem_call(kernel, [sums, *pieces], shapes, [pltpu.VMEM(shape, F32)], "level_forward")


def backward_call(planes, sums, solved, groups):
    levels = len(groups)
    count = len(groups[0])
    lower = levels - 1

    def kernel(sums, *refs):
        order = piece_order(count, planes)
        solved, refs = refs[:lower], refs[lower:]
        pieces, (out, diag, work) = [refs[i * count : (i + 1) * count] for i in range(levels)], refs[-3:]
        for i in range(count):
            split = pieces[0][i][levels * LANES : levels * LANES + DIAG_ROWS, :LANES].astype(F32)
            for level in range(levels):
                value = split[2 * level : 2 * level + 1] + split[2 * level + 1 : 2 * level + 2]
                diag[level : level + 1, at_multiple(order[i], LANES)] = value
        rows_times(pieces[-1], at_part(0), -sums[0], work, order)
        for level in range(levels, 0, -1):
            y = work if level == levels else solved[level - 1]
            value = y[...].astype(F32) / diag[level - 1 : level]
            for slot in range(levels - level):
                upper = out.at[level + slot]
                value = value - times_rows(pieces[level - 1], at_part(slot + 1), upper, order)
            work[...] = value.astype(BF16)
            out[level - 1] = times_rows(pieces[level - 1], at_part(0), work, order).astype(BF16)

    arrays = [sums, *solved, *[piece for group in groups for piece in group]]
    shape = sums.shape[1:]
    shapes = [jax.ShapeDtypeStruct((levels, *shape), BF16)]
    scratch = [pltpu.VMEM((levels, shape[1]), F32), pltpu.VMEM(shape, BF16)]
    return vmem_call(kernel, arrays, shapes, scratch, "backward")[0]


def leaf_backward_call(mask, y, inverse, couple, diag, above, groups, before, own_rows):
    blocks, levels, sep_rows, block_rows = couple.shape
    rhs_cols, width = y.shape
    planes = sep_rows // own_rows
    cols = rhs_cols // planes
    slots = [slot for group in groups for slot in group]
    size = len(groups[0]) * cols
    here = len(slots) * cols
    pair = 2 if blocks % 2 == 0 else 1
    steps = blocks // pair
    kept = len(before)

    def kernel(mask, y, inverse, couple, diag, *refs):
        pieces, refs = dict(zip(slots, refs)), refs[len(slots) + kept :]
        leaf_to, sep_to, whole, ys, leaf_out, sep_out, sems = refs
        me = places()[0]
        order = slot_blocks(planes)
        stores = []

        def store(source, target):
            stores.append(pltpu.make_async_copy(source, target, sems.at[len(stores)]))
            stores[-1].start()

        lanes = []
        for j, group in enumerate(groups):
            lanes.append(at_multiple(order[group[0]] // len(group), size))
            rows = slice(j * size, (j + 1) * size)
            ys[rows] = y[lanes[j]]
            for slot in group:
                row = j * size + lax.rem(order[slot], len(group)) * cols
                for level in range(levels):
                    whole[level, pl.ds(pl.multiple_of(row, cols), cols)] = pieces[slot][level]
        row_ids = me * own_rows + lax.broadcasted_iota(jnp.int32, (own_rows, sep_rows), 0)
        col_ids = lax.broadcasted_iota(jnp.int32, (own_rows, sep_rows), 1)
        chosen = (row_ids == col_ids).astype(F32).astype(BF16)
        for level in range(levels):
            sep_out[level] = nt(chosen, whole[level]).astype(BF16)
            for j in range(len(groups)):
                store(sep_out.at[level, :, j * size : (j + 1) * size], sep_to.at[0, level, :, lanes[j]])
        for step in range(steps):
            terms = [None] * pair
            for level in range(levels):
                weights = jnp.concatenate([couple[step * pair + b, level] for b in range(pair)], axis=1)
                value = nn(whole[level], weights)
                for b in range(pair):
                    place = slice(b * block_rows, (b + 1) * block_rows)
                    at = step * pair + b
                    term = value[:, place] * mask[level : level + 1, at : at + 1].astype(F32)
                    terms[b] = term if terms[b] is None else terms[b] + term
            for b in range(pair):
                at = step * pair + b
                place = slice(at * block_rows, (at + 1) * block_rows)
                scale = 1.0 / diag[at : at + 1]
                target = (ys[:, place].astype(F32) * scale - terms[b]).astype(BF16)
                lower = lower_unit(inverse[at].astype(F32), 0).T.astype(BF16)
                leaf_out[at] = nt(lower, target).astype(BF16)
            at = slice(step * pair, (step + 1) * pair)
            for j in range(len(groups)):
                store(leaf_out.at[at, :, j * size : (j + 1) * size], leaf_to.at[at, :, lanes[j]])
        for copy in stores:
            copy.wait()

    arrays = [mask, y, inverse, couple, diag, *[above[slot] for slot in slots], *before]
    shapes = [
        jax.ShapeDtypeStruct((blocks, block_rows, rhs_cols), BF16),
        jax.ShapeDtypeStruct((1, levels, own_rows, rhs_cols), BF16),
    ]
    scratch = [
        pltpu.VMEM((levels, here, sep_rows), BF16),
        pltpu.VMEM((here, width), BF16),
        pltpu.VMEM((blocks, block_rows, here), BF16),
        pltpu.VMEM((levels, own_rows, here), BF16),
        pltpu.SemaphoreType.DMA(((levels + steps) * len(groups),)),
    ]
    spaces = [pltpu.VMEM] * (len(arrays) - kept) + [pl.ANY] * kept
    aliases = {len(arrays) - kept + i: i for i in range(kept)}
    return kernel_call(
        kernel, arrays, spaces, shapes, scratch, "leaf_backward", out_space=pl.ANY, aliases=aliases
    )


def repacked(pieces, block_slot, parts, own_rows):
    planes, sep_rows = len(pieces), pieces[0].shape[-1]
    whole = jnp.concatenate(
        [lax.dynamic_index_in_dim(jnp.stack(pieces), block_slot[i], 0) for i in range(planes)], axis=0
    )
    count = planes * own_rows // LANES
    mats = whole[:, : parts * own_rows].reshape(count, planes // count, parts, own_rows, sep_rows)
    mats = jnp.transpose(mats, (0, 2, 1, 3, 4)).reshape(count, parts * LANES, sep_rows)
    rest = whole[:, parts * own_rows :, :own_rows]
    rest = rest.reshape(count, planes // count, rest.shape[1], own_rows)
    rest = jnp.transpose(rest, (0, 2, 1, 3)).reshape(count, rest.shape[2], LANES)
    rest = jnp.pad(rest, ((0, 0), (0, 0), (0, sep_rows - LANES)))
    mats = jnp.concatenate([mats, rest], axis=1)
    return [mats[i] for i in range(count)]


def body(
    leaf_rhs,
    leaf_inverse,
    leaf_couple,
    couple_mask,
    leaf_diag,
    sep_rhs,
    sep_inverse,
    sep_couple,
    sep_diag,
):
    levels = leaf_couple.shape[1]
    planes = lax.axis_size("plane")
    layers = lax.axis_size("layer")
    own_rows = sep_rhs.shape[1]

    own = collect_call(sep_inverse, sep_couple, sep_diag, levels, layers)
    mask = after(couple_mask.T, own[0])

    links = len(bit_orders(planes)[0])
    four = links == 2
    near = swap_link(own[0], links - 1) if four else own[0]
    quarter = planes // 4
    highs = [slot for slot in range(planes) if slot // quarter % 2 == 1]
    lows = [slot for slot in range(planes) if slot // quarter % 2 == 0]
    leaf_y, keep, send = leaf_forward_call(
        mask, [leaf_rhs, leaf_inverse], leaf_couple, sep_rhs, highs, layers
    )
    high = [after(keep, near), swap_core(send)]
    keep, send = leaf_forward_call(mask, [leaf_y], leaf_couple, sep_rhs, lows, layers)
    own_crossed = [swap_core(own[0]), swap_core(own[-1])] if four else []
    low = [after(keep, *own_crossed), swap_core(send)]
    sums, arrived = scatter_sum(low, high, [])

    def fitted(pieces, level):
        if own_rows == LANES:
            return pieces
        me = lax.axis_index("plane")
        parity = jnp.bitwise_and(jnp.bitwise_xor(me, lax.axis_index("layer")), 1)
        slots = jnp.bitwise_xor(me, jnp.asarray([slot_table(planes, 0), slot_table(planes, 1)])[parity])
        return repacked(pieces, jnp.argsort(slots).astype(jnp.int32), 1 + levels - level, own_rows)

    if four:
        near_crossed = swap_core(after(near, keep))
        side = swap_layer(near, 0)
        far = swap_link(after(near, arrived[0]), 0)
        last_own = after(own[-1], arrived[0])
        last_near = swap_link(last_own, 1)
        sums = after(sums, near_crossed, side)
        last = [own[-1], last_near, swap_link(after(last_own, arrived[1]), 0)]
    else:
        first = gather(own[0])
    groups, solved = [], []
    for level in range(1, levels + 1):
        theirs = swap_layer(sums, level - 1)
        if four and level == 1:
            theirs = after(theirs, last_near)
        sums = added_call(sums, theirs, 4_000_000_000) if level == 1 else added(sums, theirs)
        if level == 1:
            if four:
                first = [own[0], near, side, far, own_crossed[0], near_crossed, swap_core(side), swap_core(far)]
            groups.append(fitted(first, 1))
        elif four and level == levels:
            groups.append(fitted(last + [swap_core(piece) for piece in last[2:4]], level))
        else:
            groups.append(fitted(gather(own[level - 1]), level))
        if level < levels:
            y, sums = level_forward_call(planes, sums, groups[level - 1])
            solved.append(y)
        if level == 1 and four:
            last_near = after(last_near, y)
            last = last + [swap_link(last_near, 0), own_crossed[1], swap_core(last_near)]
            sums = after(sums, last[2])
    answers = backward_call(planes, sums, solved, groups)
    leaves = [mask, leaf_y, leaf_inverse, leaf_couple, leaf_diag]
    if not four or 2 * answers.shape[1] != LANES:
        above = dict(enumerate(gather(answers)))
        return tuple(leaf_backward_call(*leaves, above, [list(range(planes))], [], own_rows))
    above = dict(enumerate(gather(answers, cross=False)))
    for slot in range(3):
        above[4 + slot] = swap_core(above[slot])
    early = leaf_backward_call(*leaves, above, [[0, 4], [1, 6], [2, 5]], [], own_rows)
    above[7] = swap_core(after(above[3], early[0]))
    return tuple(leaf_backward_call(*leaves, above, [[3, 7]], early, own_rows))


def solution(mesh):
    in_specs = (
        P(("layer", "plane"), None, None),
        P(("layer", "plane"), None, None),
        P(("layer", "plane"), None, None, None),
        P(("layer", "plane"), None),
        P(("layer", "plane"), None),
        P(None, "plane", None),
        P(None, "plane", None),
        P(None, None, "plane", None),
        P(None, "plane"),
    )
    out_specs = (P(("layer", "plane"), None, None), P("layer", None, "plane", None))
    return jax.shard_map(body, mesh=mesh, in_specs=in_specs, out_specs=out_specs, check_vma=False)
```

```python
import jax
import jax.numpy as jnp
from jax import lax
from jax.experimental import pallas as pl
from jax.experimental.pallas import tpu as pltpu
from jax.sharding import PartitionSpec as P

F32 = jnp.float32
BF16 = jnp.bfloat16
LANES = 128
TILE = 256
DIAG_ROWS = 16
NT = (((1,), (1,)), ((), ()))
VMEM = pltpu.CompilerParams(vmem_limit_bytes=32 * 1024 * 1024)


def bit_orders(planes):
    link_bits = list(range(1, planes.bit_length() - 1))
    turn = len(link_bits) // 2
    return [link_bits, link_bits[turn:] + link_bits[:turn]]


def slot_table(planes, parity):
    orders = bit_orders(planes)
    count = len(orders[0])
    table = []
    for slot in range(planes):
        other = slot >> count
        block = other
        for place, bit in enumerate(orders[parity ^ other]):
            if slot >> (count - 1 - place) & 1:
                block ^= 1 << bit
        table.append(block)
    return table


def swap_core(value):
    planes = lax.axis_size("plane")
    return lax.ppermute(value, "plane", [(i, i ^ 1) for i in range(planes)])


def swap_link(value, place):
    planes, layers = lax.axis_size("plane"), lax.axis_size("layer")
    orders = bit_orders(planes)
    pairs = []
    for layer in range(layers):
        for i in range(planes):
            bit = orders[(i ^ layer) & 1][place]
            pairs.append((layer * planes + i, layer * planes + (i ^ (1 << bit))))
    return lax.ppermute(value, ("layer", "plane"), pairs)


def swap_layer(value, stride):
    layers = lax.axis_size("layer")
    return lax.ppermute(value, "layer", [(i, i ^ (1 << stride)) for i in range(layers)])


def after(value, *others):
    return lax.optimization_barrier((value, *others))[0]


def after_all(values, *others):
    return lax.optimization_barrier((*values, *others))[: len(values)]


def added(*terms):
    total = terms[0].astype(F32)
    for term in terms[1:]:
        total = total + term.astype(F32)
    return total.astype(BF16)


def scatter_sum(low, high):
    parts = list(low)
    for place in range(len(bit_orders(lax.axis_size("plane"))[0])):
        parts.append(swap_link(added(*high), place))
        low = [*low, parts[-1]]
        half = low[0].shape[0] // 2
        low, high = [term[:half] for term in low], [term[half:] for term in low]
    return parts, parts[-len(bit_orders(lax.axis_size("plane"))[0]) :]


def gather(value, cross=True):
    pieces = [value]
    for place in reversed(range(len(bit_orders(lax.axis_size("plane"))[0]))):
        pieces = pieces + [swap_link(piece, place) for piece in pieces]
    return pieces + [swap_core(piece) for piece in pieces] if cross else pieces


def lower_unit(block, first_row):
    row_count = block.shape[-2]
    col_count = block.shape[-1]
    row_ids = first_row + lax.broadcasted_iota(jnp.int32, (row_count, col_count), 0)
    col_ids = lax.broadcasted_iota(jnp.int32, (row_count, col_count), 1)
    below = jnp.where(col_ids < row_ids, block, jnp.zeros_like(block))
    return jnp.where(col_ids == row_ids, jnp.ones_like(block), below)


def nt(left, right):
    return lax.dot_general(left, right, NT, preferred_element_type=F32)


def nn(left, right):
    return jnp.dot(left, right, preferred_element_type=F32)


def places():
    return lax.axis_index("plane").astype(jnp.int32), lax.axis_index("layer").astype(jnp.int32)


def slot_blocks(planes):
    me, layer_id = places()
    parity = jnp.bitwise_and(jnp.bitwise_xor(me, layer_id), 1)
    even, odd = slot_table(planes, 0), slot_table(planes, 1)
    return [jnp.bitwise_xor(me, even[i] + parity * (odd[i] - even[i])) for i in range(planes)]


def at_multiple(index, size):
    return pl.ds(pl.multiple_of(index * size, size), size)


def sep_index(layer_id, level, layers):
    return layers - (layers >> level - 1) + jnp.right_shift(layer_id, level)


def kernel_call(kernel, arrays, spaces, out_shapes, scratch, name, flops=1, out_space=pltpu.VMEM, aliases={}):
    arrays = [
        pltpu.with_memory_space_constraint(array, space) if space == pltpu.HBM else array
        for array, space in zip(arrays, spaces)
    ]
    return pl.pallas_call(
        kernel,
        in_specs=[pl.BlockSpec(memory_space=space) for space in spaces],
        out_specs=[pl.BlockSpec(memory_space=out_space)] * len(out_shapes),
        out_shape=out_shapes,
        scratch_shapes=scratch,
        input_output_aliases=aliases,
        compiler_params=VMEM,
        cost_estimate=pl.CostEstimate(flops=flops, bytes_accessed=1, transcendentals=0),
        name=name,
    )(*arrays)


def collect_call(sep_inverse, sep_couple, sep_diag, levels, layers):
    own_rows, sep_rows = sep_inverse.shape[1:]

    def kernel(inverse, couple, diag_in, *refs):
        outs, (held, diag, sems, couple_sems) = refs[:levels], refs[levels:]
        me, layer_id = places()
        diag_load = pltpu.make_async_copy(diag_in, diag, sems.at[levels])
        diag_load.start()
        loads, moves = [], []
        for level in range(1, levels + 1):
            sep = sep_index(layer_id, level, layers)
            loads.append(pltpu.make_async_copy(inverse.at[sep], held.at[level - 1], sems.at[level - 1]))
            loads[-1].start()
            for slot in range(levels - level):
                rows = slice((slot + 1) * own_rows, (slot + 2) * own_rows)
                moves.append(
                    pltpu.make_async_copy(
                        couple.at[sep, slot], outs[level - 1].at[rows], couple_sems.at[level - 1, slot]
                    )
                )
                moves[-1].start()
        diag_load.wait()
        rows = []
        for level in range(1, levels + 1):
            value = diag[pl.ds(sep_index(layer_id, level, layers), 1)]
            high = value.astype(BF16).astype(F32)
            rows += [high, value - high]
        rows.append(jnp.zeros((DIAG_ROWS - len(rows), own_rows), F32))
        below = levels * own_rows
        outs[0][below:] = jnp.zeros((DIAG_ROWS, sep_rows), BF16)
        outs[0][below:, :own_rows] = jnp.concatenate(rows, axis=0).astype(BF16)
        for level in range(1, levels + 1):
            loads[level - 1].wait()
            lower = lower_unit(held[level - 1].astype(F32), me * own_rows)
            outs[level - 1][:own_rows] = lower.astype(BF16)
        for move in moves:
            move.wait()

    shapes = [((1 + levels - level) * own_rows, sep_rows) for level in range(1, levels + 1)]
    shapes[0] = (levels * own_rows + DIAG_ROWS, sep_rows)
    return kernel_call(
        kernel,
        [sep_inverse, sep_couple, sep_diag],
        [pltpu.HBM] * 3,
        [jax.ShapeDtypeStruct(shape, BF16) for shape in shapes],
        [
            pltpu.VMEM((levels, own_rows, sep_rows), BF16),
            pltpu.VMEM(sep_diag.shape, F32),
            pltpu.SemaphoreType.DMA((levels + 1,)),
            pltpu.SemaphoreType.DMA((levels, levels)),
        ],
        "collect",
        flops=20_000_000_000,
    )


def leaf_forward_call(mask, leaves, couple, sep_rhs, slots, layers, apart):
    first = len(leaves) == 2
    blocks, levels, sep_rows, block_rows = couple.shape
    own_rows, rhs_cols = sep_rhs.shape[1:]
    planes = sep_rows // own_rows
    cols = rhs_cols // planes
    here = len(slots) * cols
    width = blocks * block_rows
    tile = min(TILE, sep_rows)
    tiles = sep_rows // tile

    def kernel(mask, *refs):
        if first:
            rhs, inverse, couple, own_rhs, y, *parts, scaled, turned = refs
        else:
            y, couple, own_rhs, *parts, scaled, turned = refs
        me, layer_id = places()
        order = slot_blocks(planes)
        if first:
            for b in range(blocks):
                lower = lower_unit(inverse[b].astype(F32), 0).astype(BF16)
                y[:, b * block_rows : (b + 1) * block_rows] = nn(lower, rhs[b]).T.astype(BF16)
        for level in range(levels):
            alone = (jnp.bitwise_and(layer_id, (2 << level) - 1) == 0).astype(F32)
            own = own_rhs[sep_index(layer_id, level + 1, layers)].astype(F32)
            turned[...] = (own.T * -alone).astype(BF16)
            for at, slot in enumerate(slots):
                rows = slice(at * cols, (at + 1) * cols)
                scaled[level, rows, width:] = turned[at_multiple(order[slot], cols)]
                for b in range(blocks):
                    place = slice(b * block_rows, (b + 1) * block_rows)
                    used = mask[level : level + 1, b : b + 1].astype(F32).astype(BF16)
                    scaled[level, rows, place] = y[at_multiple(order[slot], cols), place] * used
        for level in range(levels):
            for t in range(tiles):
                lanes = slice(t * tile, (t + 1) * tile)
                row_ids = t * tile + lax.broadcasted_iota(jnp.int32, (tile, own_rows), 0)
                own_ids = me * own_rows + lax.broadcasted_iota(jnp.int32, (tile, own_rows), 1)
                chosen = (row_ids == own_ids).astype(F32).astype(BF16)
                weights = jnp.concatenate([couple[b, level, lanes] for b in range(blocks)] + [chosen], axis=1)
                total = nt(scaled[level], weights).astype(BF16)
                half = len(slots) // 2
                for at in range(len(slots)):
                    value = total[at * cols : (at + 1) * cols]
                    if at < half:
                        parts[0][at, level, :, lanes] = value
                    elif apart:
                        parts[1 + level][at - half, :, lanes] = value
                    else:
                        parts[1][at - half, level, :, lanes] = value

    part = jax.ShapeDtypeStruct((len(slots) // 2, levels, cols, sep_rows), BF16)
    y_shape = [jax.ShapeDtypeStruct((rhs_cols, width), BF16)] if first else []
    scratch = [pltpu.VMEM((levels, here, width + own_rows), BF16), pltpu.VMEM((rhs_cols, own_rows), BF16)]
    arrays = [mask, *leaves, couple, sep_rhs]
    one = jax.ShapeDtypeStruct((len(slots) // 2, cols, sep_rows), BF16)
    sent = [one] * levels if apart else [part]
    return vmem_call(kernel, arrays, [*y_shape, part, *sent], scratch, "leaf_forward")


def joined_call(kept, others):
    def kernel(kept, *refs):
        for level, other in enumerate(refs[:-1]):
            refs[-1][:, level] = (kept[:, level].astype(F32) + other[...].astype(F32)).astype(BF16)

    return vmem_call(kernel, [kept, *others], [jax.ShapeDtypeStruct(kept.shape, BF16)], [], "joined")[0]


def first_call(parts, seen):
    def kernel(*refs):
        total = refs[0][0].astype(F32)
        for ref in refs[1 : len(parts)]:
            total = total + ref[0].astype(F32)
        refs[-1][...] = total.astype(BF16)

    shapes = [jax.ShapeDtypeStruct(parts[0].shape[1:], BF16)]
    return vmem_call(kernel, [*parts, *seen], shapes, [], "first")[0]


def seen_call(value, flops):
    rows, lanes = min(DIAG_ROWS, value.shape[0]), min(LANES, value.shape[1])

    def kernel(value, out):
        out[...] = value[:rows, :lanes]

    shapes = [jax.ShapeDtypeStruct((rows, lanes), BF16)]
    return kernel_call(kernel, [value], [pltpu.VMEM], shapes, [], "seen", flops)[0]


def added_call(ours, theirs, flops):
    def kernel(ours, theirs, out):
        out[...] = (ours[...].astype(F32) + theirs[...].astype(F32)).astype(BF16)

    spaces = [pltpu.VMEM] * 2
    shapes = [jax.ShapeDtypeStruct(ours.shape, BF16)]
    return kernel_call(kernel, [ours, theirs], spaces, shapes, [], "added", flops)[0]


def paired(count):
    step = 2 if count % 2 == 0 else 1
    return [range(i, i + step) for i in range(0, count, step)]


def rows_times(pieces, part, vector, out, order):
    for group in paired(len(pieces)):
        rows = jnp.concatenate([pieces[i][part] for i in group], axis=0)
        result = nt(vector, rows)
        for at, i in enumerate(group):
            lanes = pl.ds(pl.multiple_of(order[i] * LANES, LANES), LANES)
            out[:, lanes] = result[:, at * LANES : (at + 1) * LANES].astype(out.dtype)


def times_rows(pieces, part, vector, order):
    total = None
    for group in paired(len(pieces)):
        rows = jnp.concatenate([pieces[i][part] for i in group], axis=0)
        left = jnp.concatenate(
            [vector[:, pl.ds(pl.multiple_of(order[i] * LANES, LANES), LANES)] for i in group], axis=1
        ).astype(BF16)
        term = nn(left, rows)
        total = term if total is None else total + term
    return total


def at_part(index):
    return slice(index * LANES, (index + 1) * LANES)


def vmem_call(kernel, arrays, out_shapes, scratch, name):
    return kernel_call(kernel, arrays, [pltpu.VMEM] * len(arrays), out_shapes, scratch, name)


def piece_order(count, planes):
    return slot_blocks(planes) if count == planes else list(range(count))


def level_forward_call(planes, sums, pieces):
    count = len(pieces)
    levels = sums.shape[0]

    def kernel(sums, *refs):
        order = piece_order(count, planes)
        pieces, (y, outs, work) = refs[:count], refs[count:]
        rows_times(pieces, at_part(0), -sums[0], y, order)
        for level in range(1, levels):
            rows_times(pieces, at_part(level), y[...], work, order)
            outs[level - 1] = (sums[level].astype(F32) + work[...]).astype(BF16)

    shape = sums.shape[1:]
    shapes = [jax.ShapeDtypeStruct(shape, BF16), jax.ShapeDtypeStruct((levels - 1, *shape), BF16)]
    return vmem_call(kernel, [sums, *pieces], shapes, [pltpu.VMEM(shape, F32)], "level_forward")


def backward_call(planes, sums, solved, groups):
    levels = len(groups)
    count = len(groups[0])
    lower = levels - 1

    def kernel(sums, *refs):
        order = piece_order(count, planes)
        solved, refs = refs[:lower], refs[lower:]
        pieces, (out, diag, work) = [refs[i * count : (i + 1) * count] for i in range(levels)], refs[-3:]
        for i in range(count):
            split = pieces[0][i][levels * LANES : levels * LANES + DIAG_ROWS, :LANES].astype(F32)
            for level in range(levels):
                value = split[2 * level : 2 * level + 1] + split[2 * level + 1 : 2 * level + 2]
                diag[level : level + 1, at_multiple(order[i], LANES)] = value
        rows_times(pieces[-1], at_part(0), -sums[0], work, order)
        for level in range(levels, 0, -1):
            y = work if level == levels else solved[level - 1]
            value = y[...].astype(F32) / diag[level - 1 : level]
            for slot in range(levels - level):
                upper = out.at[level + slot]
                value = value - times_rows(pieces[level - 1], at_part(slot + 1), upper, order)
            work[...] = value.astype(BF16)
            out[level - 1] = times_rows(pieces[level - 1], at_part(0), work, order).astype(BF16)

    arrays = [sums, *solved, *[piece for group in groups for piece in group]]
    shape = sums.shape[1:]
    shapes = [jax.ShapeDtypeStruct((levels, *shape), BF16)]
    scratch = [pltpu.VMEM((levels, shape[1]), F32), pltpu.VMEM(shape, BF16)]
    return vmem_call(kernel, arrays, shapes, scratch, "backward")[0]


def leaf_backward_call(mask, y, inverse, couple, diag, above, groups, before, own_rows):
    blocks, levels, sep_rows, block_rows = couple.shape
    rhs_cols, width = y.shape
    planes = sep_rows // own_rows
    cols = rhs_cols // planes
    slots = [slot for group in groups for slot in group]
    size = len(groups[0]) * cols
    here = len(slots) * cols
    pair = 2 if blocks % 2 == 0 else 1
    steps = blocks // pair
    kept = len(before)

    def kernel(mask, y, inverse, couple, diag, *refs):
        pieces, refs = dict(zip(slots, refs)), refs[len(slots) + kept :]
        leaf_to, sep_to, whole, ys, leaf_out, sep_out, sems = refs
        me = places()[0]
        order = slot_blocks(planes)
        stores = []

        def store(source, target):
            stores.append(pltpu.make_async_copy(source, target, sems.at[len(stores)]))
            stores[-1].start()

        lanes = []
        for j, group in enumerate(groups):
            lanes.append(at_multiple(order[group[0]] // len(group), size))
            rows = slice(j * size, (j + 1) * size)
            ys[rows] = y[lanes[j]]
            for slot in group:
                row = j * size + lax.rem(order[slot], len(group)) * cols
                for level in range(levels):
                    whole[level, pl.ds(pl.multiple_of(row, cols), cols)] = pieces[slot][level]
        row_ids = me * own_rows + lax.broadcasted_iota(jnp.int32, (own_rows, sep_rows), 0)
        col_ids = lax.broadcasted_iota(jnp.int32, (own_rows, sep_rows), 1)
        chosen = (row_ids == col_ids).astype(F32).astype(BF16)
        for level in range(levels):
            sep_out[level] = nt(chosen, whole[level]).astype(BF16)
            for j in range(len(groups)):
                store(sep_out.at[level, :, j * size : (j + 1) * size], sep_to.at[0, level, :, lanes[j]])
        for step in range(steps):
            terms = [None] * pair
            for level in range(levels):
                weights = jnp.concatenate([couple[step * pair + b, level] for b in range(pair)], axis=1)
                value = nn(whole[level], weights)
                for b in range(pair):
                    place = slice(b * block_rows, (b + 1) * block_rows)
                    at = step * pair + b
                    term = value[:, place] * mask[level : level + 1, at : at + 1].astype(F32)
                    terms[b] = term if terms[b] is None else terms[b] + term
            for b in range(pair):
                at = step * pair + b
                place = slice(at * block_rows, (at + 1) * block_rows)
                scale = 1.0 / diag[at : at + 1]
                target = (ys[:, place].astype(F32) * scale - terms[b]).astype(BF16)
                lower = lower_unit(inverse[at].astype(F32), 0).T.astype(BF16)
                leaf_out[at] = nt(lower, target).astype(BF16)
            at = slice(step * pair, (step + 1) * pair)
            for j in range(len(groups)):
                store(leaf_out.at[at, :, j * size : (j + 1) * size], leaf_to.at[at, :, lanes[j]])
        for copy in stores:
            copy.wait()

    arrays = [mask, y, inverse, couple, diag, *[above[slot] for slot in slots], *before]
    shapes = [
        jax.ShapeDtypeStruct((blocks, block_rows, rhs_cols), BF16),
        jax.ShapeDtypeStruct((1, levels, own_rows, rhs_cols), BF16),
    ]
    scratch = [
        pltpu.VMEM((levels, here, sep_rows), BF16),
        pltpu.VMEM((here, width), BF16),
        pltpu.VMEM((blocks, block_rows, here), BF16),
        pltpu.VMEM((levels, own_rows, here), BF16),
        pltpu.SemaphoreType.DMA(((levels + steps) * len(groups),)),
    ]
    spaces = [pltpu.VMEM] * (len(arrays) - kept) + [pl.ANY] * kept
    aliases = {len(arrays) - kept + i: i for i in range(kept)}
    return kernel_call(
        kernel, arrays, spaces, shapes, scratch, "leaf_backward", out_space=pl.ANY, aliases=aliases
    )


def repacked(pieces, block_slot, parts, own_rows):
    planes, sep_rows = len(pieces), pieces[0].shape[-1]
    whole = jnp.concatenate(
        [lax.dynamic_index_in_dim(jnp.stack(pieces), block_slot[i], 0) for i in range(planes)], axis=0
    )
    count = planes * own_rows // LANES
    mats = whole[:, : parts * own_rows].reshape(count, planes // count, parts, own_rows, sep_rows)
    mats = jnp.transpose(mats, (0, 2, 1, 3, 4)).reshape(count, parts * LANES, sep_rows)
    rest = whole[:, parts * own_rows :, :own_rows]
    rest = rest.reshape(count, planes // count, rest.shape[1], own_rows)
    rest = jnp.transpose(rest, (0, 2, 1, 3)).reshape(count, rest.shape[2], LANES)
    rest = jnp.pad(rest, ((0, 0), (0, 0), (0, sep_rows - LANES)))
    mats = jnp.concatenate([mats, rest], axis=1)
    return [mats[i] for i in range(count)]


def body(
    leaf_rhs,
    leaf_inverse,
    leaf_couple,
    couple_mask,
    leaf_diag,
    sep_rhs,
    sep_inverse,
    sep_couple,
    sep_diag,
):
    levels = leaf_couple.shape[1]
    planes = lax.axis_size("plane")
    layers = lax.axis_size("layer")
    own_rows = sep_rhs.shape[1]

    own = collect_call(sep_inverse, sep_couple, sep_diag, levels, layers)
    mask = after(couple_mask.T, own[0])

    links = len(bit_orders(planes)[0])
    four = links == 2
    near = swap_link(own[0], links - 1) if four else own[0]
    quarter = planes // 4
    highs = [slot for slot in range(planes) if slot // quarter % 2 == 1]
    lows = [slot for slot in range(planes) if slot // quarter % 2 == 0]
    leaf_y, keep, *send = leaf_forward_call(
        mask, [leaf_rhs, leaf_inverse], leaf_couple, sep_rhs, highs, layers, True
    )
    high = [joined_call(keep, [swap_core(part) for part in send])]
    keep, send = leaf_forward_call(mask, [leaf_y], leaf_couple, sep_rhs, lows, layers, False)
    low = [keep, swap_core(send)]
    parts, arrived = scatter_sum(low, high)
    seen = []

    def fitted(pieces, level):
        if own_rows == LANES:
            return pieces
        me = lax.axis_index("plane")
        parity = jnp.bitwise_and(jnp.bitwise_xor(me, lax.axis_index("layer")), 1)
        slots = jnp.bitwise_xor(me, jnp.asarray([slot_table(planes, 0), slot_table(planes, 1)])[parity])
        return repacked(pieces, jnp.argsort(slots).astype(jnp.int32), 1 + levels - level, own_rows)

    if four:
        own_crossed = swap_core(after(own[0], arrived[0]))
        near_crossed = swap_core(after(near, arrived[0]))
        side = swap_layer(near, 0)
        far = swap_link(after(near, arrived[0]), 0)
        last_own = after(own[-1], arrived[0])
        last_near = swap_link(last_own, 1)
        parts[0] = after(parts[0], own_crossed, near_crossed)
        seen = [seen_call(side, 3_000_000_000)]
        last = [own[-1], last_near, swap_link(after(last_own, arrived[1]), 0)]
    else:
        first = gather(own[0])
    sums = first_call(parts, seen)
    groups, solved = [], []
    for level in range(1, levels + 1):
        theirs = swap_layer(sums, level - 1)
        if four and level == 1:
            theirs = after(theirs, last_near)
        sums = added_call(sums, theirs, 4_000_000_000) if level == 1 else added(sums, theirs)
        if level == 1:
            if four:
                first = [own[0], near, side, far, own_crossed, near_crossed, swap_core(side), swap_core(far)]
            groups.append(fitted(first, 1))
        elif four and level == levels:
            groups.append(fitted(last + [swap_core(piece) for piece in last[2:4]], level))
        else:
            groups.append(fitted(gather(own[level - 1]), level))
        if level < levels:
            y, sums = level_forward_call(planes, sums, groups[level - 1])
            solved.append(y)
        if level == 1 and four:
            last_near = after(last_near, y)
            last = last + [swap_link(last_near, 0), *[swap_core(piece) for piece in after_all([last[0], last_near], y)]]
            sums = after(sums, last[2])
    answers = backward_call(planes, sums, solved, groups)
    leaves = [mask, leaf_y, leaf_inverse, leaf_couple, leaf_diag]
    if not four or 2 * answers.shape[1] != LANES:
        above = dict(enumerate(gather(answers)))
        return tuple(leaf_backward_call(*leaves, above, [list(range(planes))], [], own_rows))
    above = dict(enumerate(gather(answers, cross=False)))
    for slot in range(3):
        above[4 + slot] = swap_core(above[slot])
    early = leaf_backward_call(*leaves, above, [[0, 4], [1, 6], [2, 5]], [], own_rows)
    above[7] = swap_core(after(above[3], early[0]))
    return tuple(leaf_backward_call(*leaves, above, [[3, 7]], early, own_rows))


def solution(mesh):
    in_specs = (
        P(("layer", "plane"), None, None),
        P(("layer", "plane"), None, None),
        P(("layer", "plane"), None, None, None),
        P(("layer", "plane"), None),
        P(("layer", "plane"), None),
        P(None, "plane", None),
        P(None, "plane", None),
        P(None, None, "plane", None),
        P(None, "plane"),
    )
    out_specs = (P(("layer", "plane"), None, None), P("layer", None, "plane", None))
    return jax.shard_map(body, mesh=mesh, in_specs=in_specs, out_specs=out_specs, check_vma=False)
```

```python
import jax
import jax.numpy as jnp
from jax import lax
from jax.experimental import pallas as pl
from jax.experimental.pallas import tpu as pltpu
from jax.sharding import PartitionSpec as P

F32 = jnp.float32
BF16 = jnp.bfloat16
LANES = 128
TILE = 256
DIAG_ROWS = 16
NT = (((1,), (1,)), ((), ()))
VMEM = pltpu.CompilerParams(vmem_limit_bytes=32 * 1024 * 1024)


def bit_orders(planes):
    link_bits = list(range(1, planes.bit_length() - 1))
    turn = len(link_bits) // 2
    return [link_bits, link_bits[turn:] + link_bits[:turn]]


def slot_table(planes, parity):
    orders = bit_orders(planes)
    count = len(orders[0])
    table = []
    for slot in range(planes):
        other = slot >> count
        block = other
        for place, bit in enumerate(orders[parity ^ other]):
            if slot >> (count - 1 - place) & 1:
                block ^= 1 << bit
        table.append(block)
    return table


def swap_core(value):
    planes = lax.axis_size("plane")
    return lax.ppermute(value, "plane", [(i, i ^ 1) for i in range(planes)])


def swap_link(value, place):
    planes, layers = lax.axis_size("plane"), lax.axis_size("layer")
    orders = bit_orders(planes)
    pairs = []
    for layer in range(layers):
        for i in range(planes):
            bit = orders[(i ^ layer) & 1][place]
            pairs.append((layer * planes + i, layer * planes + (i ^ (1 << bit))))
    return lax.ppermute(value, ("layer", "plane"), pairs)


def swap_layer(value, stride):
    layers = lax.axis_size("layer")
    return lax.ppermute(value, "layer", [(i, i ^ (1 << stride)) for i in range(layers)])


def after(value, *others):
    return lax.optimization_barrier((value, *others))[0]


def after_all(values, *others):
    return lax.optimization_barrier((*values, *others))[: len(values)]


def added(*terms):
    total = terms[0].astype(F32)
    for term in terms[1:]:
        total = total + term.astype(F32)
    return total.astype(BF16)


def scatter_sum(low, high):
    parts = list(low)
    for place in range(len(bit_orders(lax.axis_size("plane"))[0])):
        parts.append(swap_link(added(*high), place))
        low = [*low, parts[-1]]
        half = low[0].shape[0] // 2
        low, high = [term[:half] for term in low], [term[half:] for term in low]
    return parts, parts[-len(bit_orders(lax.axis_size("plane"))[0]) :]


def gather(value, cross=True):
    pieces = [value]
    for place in reversed(range(len(bit_orders(lax.axis_size("plane"))[0]))):
        pieces = pieces + [swap_link(piece, place) for piece in pieces]
    return pieces + [swap_core(piece) for piece in pieces] if cross else pieces


def lower_unit(block, first_row):
    row_count = block.shape[-2]
    col_count = block.shape[-1]
    row_ids = first_row + lax.broadcasted_iota(jnp.int32, (row_count, col_count), 0)
    col_ids = lax.broadcasted_iota(jnp.int32, (row_count, col_count), 1)
    below = jnp.where(col_ids < row_ids, block, jnp.zeros_like(block))
    return jnp.where(col_ids == row_ids, jnp.ones_like(block), below)


def nt(left, right):
    return lax.dot_general(left, right, NT, preferred_element_type=F32)


def nn(left, right):
    return jnp.dot(left, right, preferred_element_type=F32)


def places():
    return lax.axis_index("plane").astype(jnp.int32), lax.axis_index("layer").astype(jnp.int32)


def slot_blocks(planes):
    me, layer_id = places()
    parity = jnp.bitwise_and(jnp.bitwise_xor(me, layer_id), 1)
    even, odd = slot_table(planes, 0), slot_table(planes, 1)
    return [jnp.bitwise_xor(me, even[i] + parity * (odd[i] - even[i])) for i in range(planes)]


def at_multiple(index, size):
    return pl.ds(pl.multiple_of(index * size, size), size)


def sep_index(layer_id, level, layers):
    return layers - (layers >> level - 1) + jnp.right_shift(layer_id, level)


def kernel_call(kernel, arrays, spaces, out_shapes, scratch, name, flops=1, out_space=pltpu.VMEM, aliases={}):
    arrays = [
        pltpu.with_memory_space_constraint(array, space) if space == pltpu.HBM else array
        for array, space in zip(arrays, spaces)
    ]
    return pl.pallas_call(
        kernel,
        in_specs=[pl.BlockSpec(memory_space=space) for space in spaces],
        out_specs=[pl.BlockSpec(memory_space=out_space)] * len(out_shapes),
        out_shape=out_shapes,
        scratch_shapes=scratch,
        input_output_aliases=aliases,
        compiler_params=VMEM,
        cost_estimate=pl.CostEstimate(flops=flops, bytes_accessed=1, transcendentals=0),
        name=name,
    )(*arrays)


def collect_call(sep_inverse, sep_couple, sep_diag, levels, layers):
    own_rows, sep_rows = sep_inverse.shape[1:]

    def kernel(inverse, couple, diag_in, *refs):
        outs, (held, diag, sems, couple_sems) = refs[:levels], refs[levels:]
        me, layer_id = places()
        diag_load = pltpu.make_async_copy(diag_in, diag, sems.at[levels])
        diag_load.start()
        loads, moves = [], []
        for level in range(1, levels + 1):
            sep = sep_index(layer_id, level, layers)
            loads.append(pltpu.make_async_copy(inverse.at[sep], held.at[level - 1], sems.at[level - 1]))
            loads[-1].start()
            for slot in range(levels - level):
                rows = slice((slot + 1) * own_rows, (slot + 2) * own_rows)
                moves.append(
                    pltpu.make_async_copy(
                        couple.at[sep, slot], outs[level - 1].at[rows], couple_sems.at[level - 1, slot]
                    )
                )
                moves[-1].start()
        diag_load.wait()
        rows = []
        for level in range(1, levels + 1):
            value = diag[pl.ds(sep_index(layer_id, level, layers), 1)]
            high = value.astype(BF16).astype(F32)
            rows += [high, value - high]
        rows.append(jnp.zeros((DIAG_ROWS - len(rows), own_rows), F32))
        below = levels * own_rows
        outs[0][below:] = jnp.zeros((DIAG_ROWS, sep_rows), BF16)
        outs[0][below:, :own_rows] = jnp.concatenate(rows, axis=0).astype(BF16)
        for level in range(1, levels + 1):
            loads[level - 1].wait()
            lower = lower_unit(held[level - 1].astype(F32), me * own_rows)
            outs[level - 1][:own_rows] = lower.astype(BF16)
        for move in moves:
            move.wait()

    shapes = [((1 + levels - level) * own_rows, sep_rows) for level in range(1, levels + 1)]
    shapes[0] = (levels * own_rows + DIAG_ROWS, sep_rows)
    return kernel_call(
        kernel,
        [sep_inverse, sep_couple, sep_diag],
        [pltpu.HBM] * 3,
        [jax.ShapeDtypeStruct(shape, BF16) for shape in shapes],
        [
            pltpu.VMEM((levels, own_rows, sep_rows), BF16),
            pltpu.VMEM(sep_diag.shape, F32),
            pltpu.SemaphoreType.DMA((levels + 1,)),
            pltpu.SemaphoreType.DMA((levels, levels)),
        ],
        "collect",
        flops=20_000_000_000,
    )


def leaf_forward_call(mask, leaves, couple, sep_rhs, slots, layers, apart):
    first = len(leaves) == 2
    blocks, levels, sep_rows, block_rows = couple.shape
    own_rows, rhs_cols = sep_rhs.shape[1:]
    planes = sep_rows // own_rows
    cols = rhs_cols // planes
    here = len(slots) * cols
    width = blocks * block_rows
    tile = min(TILE, sep_rows)
    tiles = sep_rows // tile

    def kernel(mask, *refs):
        if first:
            rhs, inverse, couple, own_rhs, y, *parts, scaled, turned = refs
        else:
            y, couple, own_rhs, *parts, scaled, turned = refs
        me, layer_id = places()
        order = slot_blocks(planes)
        if first:
            for b in range(blocks):
                lower = lower_unit(inverse[b].astype(F32), 0).astype(BF16)
                y[:, b * block_rows : (b + 1) * block_rows] = nn(lower, rhs[b]).T.astype(BF16)
        for level in range(levels):
            alone = (jnp.bitwise_and(layer_id, (2 << level) - 1) == 0).astype(F32)
            own = own_rhs[sep_index(layer_id, level + 1, layers)].astype(F32)
            turned[...] = (own.T * -alone).astype(BF16)
            for at, slot in enumerate(slots):
                rows = slice(at * cols, (at + 1) * cols)
                scaled[level, rows, width:] = turned[at_multiple(order[slot], cols)]
                for b in range(blocks):
                    place = slice(b * block_rows, (b + 1) * block_rows)
                    used = mask[level : level + 1, b : b + 1].astype(F32).astype(BF16)
                    scaled[level, rows, place] = y[at_multiple(order[slot], cols), place] * used
        for level in range(levels):
            for t in range(tiles):
                lanes = slice(t * tile, (t + 1) * tile)
                row_ids = t * tile + lax.broadcasted_iota(jnp.int32, (tile, own_rows), 0)
                own_ids = me * own_rows + lax.broadcasted_iota(jnp.int32, (tile, own_rows), 1)
                chosen = (row_ids == own_ids).astype(F32).astype(BF16)
                weights = jnp.concatenate([couple[b, level, lanes] for b in range(blocks)] + [chosen], axis=1)
                total = nt(scaled[level], weights).astype(BF16)
                half = len(slots) // 2
                for at in range(len(slots)):
                    value = total[at * cols : (at + 1) * cols]
                    if at < half:
                        parts[0][at, level, :, lanes] = value
                    elif apart:
                        parts[1 + level][at - half, :, lanes] = value
                    else:
                        parts[1][at - half, level, :, lanes] = value

    part = jax.ShapeDtypeStruct((len(slots) // 2, levels, cols, sep_rows), BF16)
    y_shape = [jax.ShapeDtypeStruct((rhs_cols, width), BF16)] if first else []
    scratch = [pltpu.VMEM((levels, here, width + own_rows), BF16), pltpu.VMEM((rhs_cols, own_rows), BF16)]
    arrays = [mask, *leaves, couple, sep_rhs]
    one = jax.ShapeDtypeStruct((len(slots) // 2, cols, sep_rows), BF16)
    sent = [one] * levels if apart else [part]
    return vmem_call(kernel, arrays, [*y_shape, part, *sent], scratch, "leaf_forward")


def joined_call(kept, others, seen):
    def kernel(kept, *refs):
        for level, other in enumerate(refs[: len(others)]):
            refs[-1][:, level] = (kept[:, level].astype(F32) + other[...].astype(F32)).astype(BF16)

    return vmem_call(kernel, [kept, *others, *seen], [jax.ShapeDtypeStruct(kept.shape, BF16)], [], "joined")[0]


def first_call(parts, seen, flops):
    def kernel(*refs):
        total = refs[0][0].astype(F32)
        for ref in refs[1 : len(parts)]:
            total = total + ref[0].astype(F32)
        refs[-1][...] = total.astype(BF16)

    shapes = [jax.ShapeDtypeStruct(parts[0].shape[1:], BF16)]
    arrays = [*parts, *seen]
    return kernel_call(kernel, arrays, [pltpu.VMEM] * len(arrays), shapes, [], "first", flops)[0]


def seen_call(value, flops):
    rows, lanes = min(DIAG_ROWS, value.shape[0]), min(LANES, value.shape[1])

    def kernel(value, out):
        out[...] = value[:rows, :lanes]

    shapes = [jax.ShapeDtypeStruct((rows, lanes), BF16)]
    return kernel_call(kernel, [value], [pltpu.VMEM], shapes, [], "seen", flops)[0]


def added_call(ours, theirs, flops):
    def kernel(ours, theirs, out):
        out[...] = (ours[...].astype(F32) + theirs[...].astype(F32)).astype(BF16)

    spaces = [pltpu.VMEM] * 2
    shapes = [jax.ShapeDtypeStruct(ours.shape, BF16)]
    return kernel_call(kernel, [ours, theirs], spaces, shapes, [], "added", flops)[0]


def paired(count):
    step = 2 if count % 2 == 0 else 1
    return [range(i, i + step) for i in range(0, count, step)]


def rows_times(pieces, part, vector, out, order):
    for group in paired(len(pieces)):
        rows = jnp.concatenate([pieces[i][part] for i in group], axis=0)
        result = nt(vector, rows)
        for at, i in enumerate(group):
            lanes = pl.ds(pl.multiple_of(order[i] * LANES, LANES), LANES)
            out[:, lanes] = result[:, at * LANES : (at + 1) * LANES].astype(out.dtype)


def times_rows(pieces, part, vector, order):
    total = None
    for group in paired(len(pieces)):
        rows = jnp.concatenate([pieces[i][part] for i in group], axis=0)
        left = jnp.concatenate(
            [vector[:, pl.ds(pl.multiple_of(order[i] * LANES, LANES), LANES)] for i in group], axis=1
        ).astype(BF16)
        term = nn(left, rows)
        total = term if total is None else total + term
    return total


def at_part(index):
    return slice(index * LANES, (index + 1) * LANES)


def vmem_call(kernel, arrays, out_shapes, scratch, name):
    return kernel_call(kernel, arrays, [pltpu.VMEM] * len(arrays), out_shapes, scratch, name)


def piece_order(count, planes):
    return slot_blocks(planes) if count == planes else list(range(count))


def level_forward_call(planes, sums, pieces):
    count = len(pieces)
    levels = sums.shape[0]

    def kernel(sums, *refs):
        order = piece_order(count, planes)
        pieces, (y, outs, work) = refs[:count], refs[count:]
        rows_times(pieces, at_part(0), -sums[0], y, order)
        for level in range(1, levels):
            rows_times(pieces, at_part(level), y[...], work, order)
            outs[level - 1] = (sums[level].astype(F32) + work[...]).astype(BF16)

    shape = sums.shape[1:]
    shapes = [jax.ShapeDtypeStruct(shape, BF16), jax.ShapeDtypeStruct((levels - 1, *shape), BF16)]
    return vmem_call(kernel, [sums, *pieces], shapes, [pltpu.VMEM(shape, F32)], "level_forward")


def backward_call(planes, sums, solved, groups):
    levels = len(groups)
    count = len(groups[0])
    lower = levels - 1

    def kernel(sums, *refs):
        order = piece_order(count, planes)
        solved, refs = refs[:lower], refs[lower:]
        pieces, (out, diag, work) = [refs[i * count : (i + 1) * count] for i in range(levels)], refs[-3:]
        for i in range(count):
            split = pieces[0][i][levels * LANES : levels * LANES + DIAG_ROWS, :LANES].astype(F32)
            for level in range(levels):
                value = split[2 * level : 2 * level + 1] + split[2 * level + 1 : 2 * level + 2]
                diag[level : level + 1, at_multiple(order[i], LANES)] = value
        rows_times(pieces[-1], at_part(0), -sums[0], work, order)
        for level in range(levels, 0, -1):
            y = work if level == levels else solved[level - 1]
            value = y[...].astype(F32) / diag[level - 1 : level]
            for slot in range(levels - level):
                upper = out.at[level + slot]
                value = value - times_rows(pieces[level - 1], at_part(slot + 1), upper, order)
            work[...] = value.astype(BF16)
            out[level - 1] = times_rows(pieces[level - 1], at_part(0), work, order).astype(BF16)

    arrays = [sums, *solved, *[piece for group in groups for piece in group]]
    shape = sums.shape[1:]
    shapes = [jax.ShapeDtypeStruct((levels, *shape), BF16)]
    scratch = [pltpu.VMEM((levels, shape[1]), F32), pltpu.VMEM(shape, BF16)]
    return vmem_call(kernel, arrays, shapes, scratch, "backward")[0]


def leaf_backward_call(mask, y, inverse, couple, diag, above, groups, before, own_rows):
    blocks, levels, sep_rows, block_rows = couple.shape
    rhs_cols, width = y.shape
    planes = sep_rows // own_rows
    cols = rhs_cols // planes
    slots = [slot for group in groups for slot in group]
    size = len(groups[0]) * cols
    here = len(slots) * cols
    pair = 2 if blocks % 2 == 0 else 1
    steps = blocks // pair
    kept = len(before)

    def kernel(mask, y, inverse, couple, diag, *refs):
        pieces, refs = dict(zip(slots, refs)), refs[len(slots) + kept :]
        leaf_to, sep_to, whole, ys, leaf_out, sep_out, sems = refs
        me = places()[0]
        order = slot_blocks(planes)
        stores = []

        def store(source, target):
            stores.append(pltpu.make_async_copy(source, target, sems.at[len(stores)]))
            stores[-1].start()

        lanes = []
        for j, group in enumerate(groups):
            lanes.append(at_multiple(order[group[0]] // len(group), size))
            rows = slice(j * size, (j + 1) * size)
            ys[rows] = y[lanes[j]]
            for slot in group:
                row = j * size + lax.rem(order[slot], len(group)) * cols
                for level in range(levels):
                    whole[level, pl.ds(pl.multiple_of(row, cols), cols)] = pieces[slot][level]
        row_ids = me * own_rows + lax.broadcasted_iota(jnp.int32, (own_rows, sep_rows), 0)
        col_ids = lax.broadcasted_iota(jnp.int32, (own_rows, sep_rows), 1)
        chosen = (row_ids == col_ids).astype(F32).astype(BF16)
        for level in range(levels):
            sep_out[level] = nt(chosen, whole[level]).astype(BF16)
            for j in range(len(groups)):
                store(sep_out.at[level, :, j * size : (j + 1) * size], sep_to.at[0, level, :, lanes[j]])
        for step in range(steps):
            terms = [None] * pair
            for level in range(levels):
                weights = jnp.concatenate([couple[step * pair + b, level] for b in range(pair)], axis=1)
                value = nn(whole[level], weights)
                for b in range(pair):
                    place = slice(b * block_rows, (b + 1) * block_rows)
                    at = step * pair + b
                    term = value[:, place] * mask[level : level + 1, at : at + 1].astype(F32)
                    terms[b] = term if terms[b] is None else terms[b] + term
            for b in range(pair):
                at = step * pair + b
                place = slice(at * block_rows, (at + 1) * block_rows)
                scale = 1.0 / diag[at : at + 1]
                target = (ys[:, place].astype(F32) * scale - terms[b]).astype(BF16)
                lower = lower_unit(inverse[at].astype(F32), 0).T.astype(BF16)
                leaf_out[at] = nt(lower, target).astype(BF16)
            at = slice(step * pair, (step + 1) * pair)
            for j in range(len(groups)):
                store(leaf_out.at[at, :, j * size : (j + 1) * size], leaf_to.at[at, :, lanes[j]])
        for copy in stores:
            copy.wait()

    arrays = [mask, y, inverse, couple, diag, *[above[slot] for slot in slots], *before]
    shapes = [
        jax.ShapeDtypeStruct((blocks, block_rows, rhs_cols), BF16),
        jax.ShapeDtypeStruct((1, levels, own_rows, rhs_cols), BF16),
    ]
    scratch = [
        pltpu.VMEM((levels, here, sep_rows), BF16),
        pltpu.VMEM((here, width), BF16),
        pltpu.VMEM((blocks, block_rows, here), BF16),
        pltpu.VMEM((levels, own_rows, here), BF16),
        pltpu.SemaphoreType.DMA(((levels + steps) * len(groups),)),
    ]
    spaces = [pltpu.VMEM] * (len(arrays) - kept) + [pl.ANY] * kept
    aliases = {len(arrays) - kept + i: i for i in range(kept)}
    return kernel_call(
        kernel, arrays, spaces, shapes, scratch, "leaf_backward", out_space=pl.ANY, aliases=aliases
    )


def repacked(pieces, block_slot, parts, own_rows):
    planes, sep_rows = len(pieces), pieces[0].shape[-1]
    whole = jnp.concatenate(
        [lax.dynamic_index_in_dim(jnp.stack(pieces), block_slot[i], 0) for i in range(planes)], axis=0
    )
    count = planes * own_rows // LANES
    mats = whole[:, : parts * own_rows].reshape(count, planes // count, parts, own_rows, sep_rows)
    mats = jnp.transpose(mats, (0, 2, 1, 3, 4)).reshape(count, parts * LANES, sep_rows)
    rest = whole[:, parts * own_rows :, :own_rows]
    rest = rest.reshape(count, planes // count, rest.shape[1], own_rows)
    rest = jnp.transpose(rest, (0, 2, 1, 3)).reshape(count, rest.shape[2], LANES)
    rest = jnp.pad(rest, ((0, 0), (0, 0), (0, sep_rows - LANES)))
    mats = jnp.concatenate([mats, rest], axis=1)
    return [mats[i] for i in range(count)]


def body(
    leaf_rhs,
    leaf_inverse,
    leaf_couple,
    couple_mask,
    leaf_diag,
    sep_rhs,
    sep_inverse,
    sep_couple,
    sep_diag,
):
    levels = leaf_couple.shape[1]
    planes = lax.axis_size("plane")
    layers = lax.axis_size("layer")
    own_rows = sep_rhs.shape[1]

    own = collect_call(sep_inverse, sep_couple, sep_diag, levels, layers)
    mask = after(couple_mask.T, own[0])

    links = len(bit_orders(planes)[0])
    four = links == 2
    near = swap_link(own[0], links - 1) if four else own[0]
    quarter = planes // 4
    highs = [slot for slot in range(planes) if slot // quarter % 2 == 1]
    lows = [slot for slot in range(planes) if slot // quarter % 2 == 0]
    leaf_y, keep, *send = leaf_forward_call(
        mask, [leaf_rhs, leaf_inverse], leaf_couple, sep_rhs, highs, layers, True
    )
    own_crossed = [swap_core(own[0])] if four else []
    high = [joined_call(keep, [swap_core(part) for part in send], own_crossed)]
    keep, send = leaf_forward_call(mask, [leaf_y], leaf_couple, sep_rhs, lows, layers, False)
    low = [keep, swap_core(send)]
    parts, arrived = scatter_sum(low, high)
    seen = []

    def fitted(pieces, level):
        if own_rows == LANES:
            return pieces
        me = lax.axis_index("plane")
        parity = jnp.bitwise_and(jnp.bitwise_xor(me, lax.axis_index("layer")), 1)
        slots = jnp.bitwise_xor(me, jnp.asarray([slot_table(planes, 0), slot_table(planes, 1)])[parity])
        return repacked(pieces, jnp.argsort(slots).astype(jnp.int32), 1 + levels - level, own_rows)

    if four:
        near_crossed = swap_core(after(near, arrived[0]))
        side = swap_layer(near, 0)
        far = swap_link(after(near, arrived[0]), 0)
        last_own = after(own[-1], arrived[0])
        last_near = swap_link(last_own, 1)
        parts[0] = after(parts[0], near_crossed)
        seen = [seen_call(side, 3_000_000_000)]
        last = [own[-1], last_near, swap_link(after(last_own, arrived[1]), 0)]
    else:
        first = gather(own[0])
    sums = first_call(parts, seen, 1)
    groups, solved = [], []
    for level in range(1, levels + 1):
        theirs = swap_layer(sums, level - 1)
        if four and level == 1:
            theirs = after(theirs, last_near)
        sums = added_call(sums, theirs, 4_000_000_000) if level == 1 else added(sums, theirs)
        if level == 1:
            if four:
                first = [own[0], near, side, far, own_crossed[0], near_crossed, swap_core(side), swap_core(far)]
            groups.append(fitted(first, 1))
        elif four and level == levels:
            groups.append(fitted(last + [swap_core(piece) for piece in last[2:4]], level))
        else:
            groups.append(fitted(gather(own[level - 1]), level))
        if level < levels:
            y, sums = level_forward_call(planes, sums, groups[level - 1])
            solved.append(y)
        if level == 1 and four:
            last = last + [swap_link(last_near, 0), *[swap_core(piece) for piece in after_all([last[0], last_near], y)]]
    answers = backward_call(planes, sums, solved, groups)
    leaves = [mask, leaf_y, leaf_inverse, leaf_couple, leaf_diag]
    if not four or 2 * answers.shape[1] != LANES:
        above = dict(enumerate(gather(answers)))
        return tuple(leaf_backward_call(*leaves, above, [list(range(planes))], [], own_rows))
    above = dict(enumerate(gather(answers, cross=False)))
    for slot in range(3):
        above[4 + slot] = swap_core(above[slot])
    early = leaf_backward_call(*leaves, above, [[0, 4], [1, 6], [2, 5]], [], own_rows)
    above[7] = swap_core(after(above[3], early[0]))
    return tuple(leaf_backward_call(*leaves, above, [[3, 7]], early, own_rows))


def solution(mesh):
    in_specs = (
        P(("layer", "plane"), None, None),
        P(("layer", "plane"), None, None),
        P(("layer", "plane"), None, None, None),
        P(("layer", "plane"), None),
        P(("layer", "plane"), None),
        P(None, "plane", None),
        P(None, "plane", None),
        P(None, None, "plane", None),
        P(None, "plane"),
    )
    out_specs = (P(("layer", "plane"), None, None), P("layer", None, "plane", None))
    return jax.shard_map(body, mesh=mesh, in_specs=in_specs, out_specs=out_specs, check_vma=False)
```

```python
import jax
import jax.numpy as jnp
from jax import lax
from jax.experimental import pallas as pl
from jax.experimental.pallas import tpu as pltpu
from jax.sharding import PartitionSpec as P

F32 = jnp.float32
BF16 = jnp.bfloat16
LANES = 128
TILE = 256
DIAG_ROWS = 16
NT = (((1,), (1,)), ((), ()))
VMEM = pltpu.CompilerParams(vmem_limit_bytes=32 * 1024 * 1024)


def bit_orders(planes):
    link_bits = list(range(1, planes.bit_length() - 1))
    turn = len(link_bits) // 2
    return [link_bits, link_bits[turn:] + link_bits[:turn]]


def slot_table(planes, parity):
    orders = bit_orders(planes)
    count = len(orders[0])
    table = []
    for slot in range(planes):
        other = slot >> count
        block = other
        for place, bit in enumerate(orders[parity ^ other]):
            if slot >> (count - 1 - place) & 1:
                block ^= 1 << bit
        table.append(block)
    return table


def swap_core(value):
    planes = lax.axis_size("plane")
    return lax.ppermute(value, "plane", [(i, i ^ 1) for i in range(planes)])


def swap_link(value, place):
    planes, layers = lax.axis_size("plane"), lax.axis_size("layer")
    orders = bit_orders(planes)
    pairs = []
    for layer in range(layers):
        for i in range(planes):
            bit = orders[(i ^ layer) & 1][place]
            pairs.append((layer * planes + i, layer * planes + (i ^ (1 << bit))))
    return lax.ppermute(value, ("layer", "plane"), pairs)


def swap_layer(value, stride):
    layers = lax.axis_size("layer")
    return lax.ppermute(value, "layer", [(i, i ^ (1 << stride)) for i in range(layers)])


def after(value, *others):
    return lax.optimization_barrier((value, *others))[0]


def after_all(values, *others):
    return lax.optimization_barrier((*values, *others))[: len(values)]


def added(*terms):
    total = terms[0].astype(F32)
    for term in terms[1:]:
        total = total + term.astype(F32)
    return total.astype(BF16)


def scatter_sum(low, high):
    parts = list(low)
    for place in range(len(bit_orders(lax.axis_size("plane"))[0])):
        parts.append(swap_link(added(*high), place))
        low = [*low, parts[-1]]
        half = low[0].shape[0] // 2
        low, high = [term[:half] for term in low], [term[half:] for term in low]
    return parts, parts[-len(bit_orders(lax.axis_size("plane"))[0]) :]


def gather(value, cross=True):
    pieces = [value]
    for place in reversed(range(len(bit_orders(lax.axis_size("plane"))[0]))):
        pieces = pieces + [swap_link(piece, place) for piece in pieces]
    return pieces + [swap_core(piece) for piece in pieces] if cross else pieces


def lower_unit(block, first_row):
    row_count = block.shape[-2]
    col_count = block.shape[-1]
    row_ids = first_row + lax.broadcasted_iota(jnp.int32, (row_count, col_count), 0)
    col_ids = lax.broadcasted_iota(jnp.int32, (row_count, col_count), 1)
    below = jnp.where(col_ids < row_ids, block, jnp.zeros_like(block))
    return jnp.where(col_ids == row_ids, jnp.ones_like(block), below)


def nt(left, right):
    return lax.dot_general(left, right, NT, preferred_element_type=F32)


def nn(left, right):
    return jnp.dot(left, right, preferred_element_type=F32)


def places():
    return lax.axis_index("plane").astype(jnp.int32), lax.axis_index("layer").astype(jnp.int32)


def slot_blocks(planes):
    me, layer_id = places()
    parity = jnp.bitwise_and(jnp.bitwise_xor(me, layer_id), 1)
    even, odd = slot_table(planes, 0), slot_table(planes, 1)
    return [jnp.bitwise_xor(me, even[i] + parity * (odd[i] - even[i])) for i in range(planes)]


def at_multiple(index, size):
    return pl.ds(pl.multiple_of(index * size, size), size)


def sep_index(layer_id, level, layers):
    return layers - (layers >> level - 1) + jnp.right_shift(layer_id, level)


def kernel_call(kernel, arrays, spaces, out_shapes, scratch, name, flops=1, out_space=pltpu.VMEM, aliases={}):
    arrays = [
        pltpu.with_memory_space_constraint(array, space) if space == pltpu.HBM else array
        for array, space in zip(arrays, spaces)
    ]
    return pl.pallas_call(
        kernel,
        in_specs=[pl.BlockSpec(memory_space=space) for space in spaces],
        out_specs=[pl.BlockSpec(memory_space=out_space)] * len(out_shapes),
        out_shape=out_shapes,
        scratch_shapes=scratch,
        input_output_aliases=aliases,
        compiler_params=VMEM,
        cost_estimate=pl.CostEstimate(flops=flops, bytes_accessed=1, transcendentals=0),
        name=name,
    )(*arrays)


def collect_call(sep_inverse, sep_couple, sep_diag, levels, layers):
    own_rows, sep_rows = sep_inverse.shape[1:]

    def kernel(inverse, couple, diag_in, *refs):
        outs, (held, diag, sems, couple_sems) = refs[:levels], refs[levels:]
        me, layer_id = places()
        diag_load = pltpu.make_async_copy(diag_in, diag, sems.at[levels])
        diag_load.start()
        loads, moves = [], []
        for level in range(1, levels + 1):
            sep = sep_index(layer_id, level, layers)
            loads.append(pltpu.make_async_copy(inverse.at[sep], held.at[level - 1], sems.at[level - 1]))
            loads[-1].start()
            for slot in range(levels - level):
                rows = slice((slot + 1) * own_rows, (slot + 2) * own_rows)
                moves.append(
                    pltpu.make_async_copy(
                        couple.at[sep, slot], outs[level - 1].at[rows], couple_sems.at[level - 1, slot]
                    )
                )
                moves[-1].start()
        diag_load.wait()
        rows = []
        for level in range(1, levels + 1):
            value = diag[pl.ds(sep_index(layer_id, level, layers), 1)]
            high = value.astype(BF16).astype(F32)
            rows += [high, value - high]
        rows.append(jnp.zeros((DIAG_ROWS - len(rows), own_rows), F32))
        outs[-1][own_rows:] = jnp.zeros((DIAG_ROWS, sep_rows), BF16)
        outs[-1][own_rows:, :own_rows] = jnp.concatenate(rows, axis=0).astype(BF16)
        for level in range(1, levels + 1):
            loads[level - 1].wait()
            lower = lower_unit(held[level - 1].astype(F32), me * own_rows)
            outs[level - 1][:own_rows] = lower.astype(BF16)
        for move in moves:
            move.wait()

    shapes = [((1 + levels - level) * own_rows, sep_rows) for level in range(1, levels + 1)]
    shapes[-1] = (own_rows + DIAG_ROWS, sep_rows)
    return kernel_call(
        kernel,
        [sep_inverse, sep_couple, sep_diag],
        [pltpu.HBM] * 3,
        [jax.ShapeDtypeStruct(shape, BF16) for shape in shapes],
        [
            pltpu.VMEM((levels, own_rows, sep_rows), BF16),
            pltpu.VMEM(sep_diag.shape, F32),
            pltpu.SemaphoreType.DMA((levels + 1,)),
            pltpu.SemaphoreType.DMA((levels, levels)),
        ],
        "collect",
        flops=20_000_000_000,
    )


def leaf_forward_call(mask, leaves, couple, sep_rhs, slots, layers, apart):
    first = len(leaves) == 2
    blocks, levels, sep_rows, block_rows = couple.shape
    own_rows, rhs_cols = sep_rhs.shape[1:]
    planes = sep_rows // own_rows
    cols = rhs_cols // planes
    here = len(slots) * cols
    width = blocks * block_rows
    tile = min(TILE, sep_rows)
    tiles = sep_rows // tile

    def kernel(mask, *refs):
        if first:
            rhs, inverse, couple, own_rhs, y, *parts, scaled, turned = refs
        else:
            y, couple, own_rhs, *parts, scaled, turned = refs
        me, layer_id = places()
        order = slot_blocks(planes)
        if first:
            for b in range(blocks):
                lower = lower_unit(inverse[b].astype(F32), 0).astype(BF16)
                y[:, b * block_rows : (b + 1) * block_rows] = nn(lower, rhs[b]).T.astype(BF16)
        for level in range(levels):
            alone = (jnp.bitwise_and(layer_id, (2 << level) - 1) == 0).astype(F32)
            own = own_rhs[sep_index(layer_id, level + 1, layers)].astype(F32)
            turned[...] = (own.T * -alone).astype(BF16)
            for at, slot in enumerate(slots):
                rows = slice(at * cols, (at + 1) * cols)
                scaled[level, rows, width:] = turned[at_multiple(order[slot], cols)]
                for b in range(blocks):
                    place = slice(b * block_rows, (b + 1) * block_rows)
                    used = mask[level : level + 1, b : b + 1].astype(F32).astype(BF16)
                    scaled[level, rows, place] = y[at_multiple(order[slot], cols), place] * used
        for level in range(levels):
            for t in range(tiles):
                lanes = slice(t * tile, (t + 1) * tile)
                row_ids = t * tile + lax.broadcasted_iota(jnp.int32, (tile, own_rows), 0)
                own_ids = me * own_rows + lax.broadcasted_iota(jnp.int32, (tile, own_rows), 1)
                chosen = (row_ids == own_ids).astype(F32).astype(BF16)
                weights = jnp.concatenate([couple[b, level, lanes] for b in range(blocks)] + [chosen], axis=1)
                total = nt(scaled[level], weights).astype(BF16)
                half = len(slots) // 2
                for at in range(len(slots)):
                    value = total[at * cols : (at + 1) * cols]
                    if at < half:
                        parts[0][at, level, :, lanes] = value
                    elif apart:
                        parts[1 + level][at - half, :, lanes] = value
                    else:
                        parts[1][at - half, level, :, lanes] = value

    part = jax.ShapeDtypeStruct((len(slots) // 2, levels, cols, sep_rows), BF16)
    y_shape = [jax.ShapeDtypeStruct((rhs_cols, width), BF16)] if first else []
    scratch = [pltpu.VMEM((levels, here, width + own_rows), BF16), pltpu.VMEM((rhs_cols, own_rows), BF16)]
    arrays = [mask, *leaves, couple, sep_rhs]
    one = jax.ShapeDtypeStruct((len(slots) // 2, cols, sep_rows), BF16)
    sent = [one] * levels if apart else [part]
    return vmem_call(kernel, arrays, [*y_shape, part, *sent], scratch, "leaf_forward")


def joined_call(kept, others, seen):
    def kernel(kept, *refs):
        for level, other in enumerate(refs[: len(others)]):
            refs[-1][:, level] = (kept[:, level].astype(F32) + other[...].astype(F32)).astype(BF16)

    return vmem_call(kernel, [kept, *others, *seen], [jax.ShapeDtypeStruct(kept.shape, BF16)], [], "joined")[0]


def first_call(parts, seen, flops):
    def kernel(*refs):
        total = refs[0][0].astype(F32)
        for ref in refs[1 : len(parts)]:
            total = total + ref[0].astype(F32)
        refs[-1][...] = total.astype(BF16)

    shapes = [jax.ShapeDtypeStruct(parts[0].shape[1:], BF16)]
    arrays = [*parts, *seen]
    return kernel_call(kernel, arrays, [pltpu.VMEM] * len(arrays), shapes, [], "first", flops)[0]


def seen_call(value, flops):
    rows, lanes = min(DIAG_ROWS, value.shape[0]), min(LANES, value.shape[1])

    def kernel(value, out):
        out[...] = value[:rows, :lanes]

    shapes = [jax.ShapeDtypeStruct((rows, lanes), BF16)]
    return kernel_call(kernel, [value], [pltpu.VMEM], shapes, [], "seen", flops)[0]


def added_call(ours, theirs, seen, flops):
    def kernel(ours, theirs, *refs):
        refs[-1][...] = (ours[...].astype(F32) + theirs[...].astype(F32)).astype(BF16)

    arrays = [ours, theirs, *seen]
    shapes = [jax.ShapeDtypeStruct(ours.shape, BF16)]
    return kernel_call(kernel, arrays, [pltpu.VMEM] * len(arrays), shapes, [], "added", flops)[0]


def paired(count):
    step = 2 if count % 2 == 0 else 1
    return [range(i, i + step) for i in range(0, count, step)]


def rows_times(pieces, part, vector, out, order):
    for group in paired(len(pieces)):
        rows = jnp.concatenate([pieces[i][part] for i in group], axis=0)
        result = nt(vector, rows)
        for at, i in enumerate(group):
            lanes = pl.ds(pl.multiple_of(order[i] * LANES, LANES), LANES)
            out[:, lanes] = result[:, at * LANES : (at + 1) * LANES].astype(out.dtype)


def times_rows(pieces, part, vector, order):
    total = None
    for group in paired(len(pieces)):
        rows = jnp.concatenate([pieces[i][part] for i in group], axis=0)
        left = jnp.concatenate(
            [vector[:, pl.ds(pl.multiple_of(order[i] * LANES, LANES), LANES)] for i in group], axis=1
        ).astype(BF16)
        term = nn(left, rows)
        total = term if total is None else total + term
    return total


def at_part(index):
    return slice(index * LANES, (index + 1) * LANES)


def vmem_call(kernel, arrays, out_shapes, scratch, name):
    return kernel_call(kernel, arrays, [pltpu.VMEM] * len(arrays), out_shapes, scratch, name)


def piece_order(count, planes):
    return slot_blocks(planes) if count == planes else list(range(count))


def level_forward_call(planes, sums, pieces):
    count = len(pieces)
    levels = sums.shape[0]

    def kernel(sums, *refs):
        order = piece_order(count, planes)
        pieces, (y, outs, work) = refs[:count], refs[count:]
        rows_times(pieces, at_part(0), -sums[0], y, order)
        for level in range(1, levels):
            rows_times(pieces, at_part(level), y[...], work, order)
            outs[level - 1] = (sums[level].astype(F32) + work[...]).astype(BF16)

    shape = sums.shape[1:]
    shapes = [jax.ShapeDtypeStruct(shape, BF16), jax.ShapeDtypeStruct((levels - 1, *shape), BF16)]
    return vmem_call(kernel, [sums, *pieces], shapes, [pltpu.VMEM(shape, F32)], "level_forward")


def backward_call(planes, sums, solved, groups):
    levels = len(groups)
    count = len(groups[0])
    lower = levels - 1

    def kernel(sums, *refs):
        order = piece_order(count, planes)
        solved, refs = refs[:lower], refs[lower:]
        pieces, (out, diag, work) = [refs[i * count : (i + 1) * count] for i in range(levels)], refs[-3:]
        for i in range(count):
            split = pieces[-1][i][LANES : LANES + DIAG_ROWS, :LANES].astype(F32)
            for level in range(levels):
                value = split[2 * level : 2 * level + 1] + split[2 * level + 1 : 2 * level + 2]
                diag[level : level + 1, at_multiple(order[i], LANES)] = value
        rows_times(pieces[-1], at_part(0), -sums[0], work, order)
        for level in range(levels, 0, -1):
            y = work if level == levels else solved[level - 1]
            value = y[...].astype(F32) / diag[level - 1 : level]
            for slot in range(levels - level):
                upper = out.at[level + slot]
                value = value - times_rows(pieces[level - 1], at_part(slot + 1), upper, order)
            work[...] = value.astype(BF16)
            out[level - 1] = times_rows(pieces[level - 1], at_part(0), work, order).astype(BF16)

    arrays = [sums, *solved, *[piece for group in groups for piece in group]]
    shape = sums.shape[1:]
    shapes = [jax.ShapeDtypeStruct((levels, *shape), BF16)]
    scratch = [pltpu.VMEM((levels, shape[1]), F32), pltpu.VMEM(shape, BF16)]
    return vmem_call(kernel, arrays, shapes, scratch, "backward")[0]


def leaf_backward_call(mask, y, inverse, couple, diag, above, groups, before, own_rows):
    blocks, levels, sep_rows, block_rows = couple.shape
    rhs_cols, width = y.shape
    planes = sep_rows // own_rows
    cols = rhs_cols // planes
    slots = [slot for group in groups for slot in group]
    size = len(groups[0]) * cols
    here = len(slots) * cols
    pair = 2 if blocks % 2 == 0 else 1
    steps = blocks // pair
    kept = len(before)

    def kernel(mask, y, inverse, couple, diag, *refs):
        pieces, refs = dict(zip(slots, refs)), refs[len(slots) + kept :]
        leaf_to, sep_to, whole, ys, leaf_out, sep_out, sems = refs
        me = places()[0]
        order = slot_blocks(planes)
        stores = []

        def store(source, target):
            stores.append(pltpu.make_async_copy(source, target, sems.at[len(stores)]))
            stores[-1].start()

        lanes = []
        for j, group in enumerate(groups):
            lanes.append(at_multiple(order[group[0]] // len(group), size))
            rows = slice(j * size, (j + 1) * size)
            ys[rows] = y[lanes[j]]
            for slot in group:
                row = j * size + lax.rem(order[slot], len(group)) * cols
                for level in range(levels):
                    whole[level, pl.ds(pl.multiple_of(row, cols), cols)] = pieces[slot][level]
        row_ids = me * own_rows + lax.broadcasted_iota(jnp.int32, (own_rows, sep_rows), 0)
        col_ids = lax.broadcasted_iota(jnp.int32, (own_rows, sep_rows), 1)
        chosen = (row_ids == col_ids).astype(F32).astype(BF16)
        for level in range(levels):
            sep_out[level] = nt(chosen, whole[level]).astype(BF16)
            for j in range(len(groups)):
                store(sep_out.at[level, :, j * size : (j + 1) * size], sep_to.at[0, level, :, lanes[j]])
        for step in range(steps):
            terms = [None] * pair
            for level in range(levels):
                weights = jnp.concatenate([couple[step * pair + b, level] for b in range(pair)], axis=1)
                value = nn(whole[level], weights)
                for b in range(pair):
                    place = slice(b * block_rows, (b + 1) * block_rows)
                    at = step * pair + b
                    term = value[:, place] * mask[level : level + 1, at : at + 1].astype(F32)
                    terms[b] = term if terms[b] is None else terms[b] + term
            for b in range(pair):
                at = step * pair + b
                place = slice(at * block_rows, (at + 1) * block_rows)
                scale = 1.0 / diag[at : at + 1]
                target = (ys[:, place].astype(F32) * scale - terms[b]).astype(BF16)
                lower = lower_unit(inverse[at].astype(F32), 0).T.astype(BF16)
                leaf_out[at] = nt(lower, target).astype(BF16)
            at = slice(step * pair, (step + 1) * pair)
            for j in range(len(groups)):
                store(leaf_out.at[at, :, j * size : (j + 1) * size], leaf_to.at[at, :, lanes[j]])
        for copy in stores:
            copy.wait()

    arrays = [mask, y, inverse, couple, diag, *[above[slot] for slot in slots], *before]
    shapes = [
        jax.ShapeDtypeStruct((blocks, block_rows, rhs_cols), BF16),
        jax.ShapeDtypeStruct((1, levels, own_rows, rhs_cols), BF16),
    ]
    scratch = [
        pltpu.VMEM((levels, here, sep_rows), BF16),
        pltpu.VMEM((here, width), BF16),
        pltpu.VMEM((blocks, block_rows, here), BF16),
        pltpu.VMEM((levels, own_rows, here), BF16),
        pltpu.SemaphoreType.DMA(((levels + steps) * len(groups),)),
    ]
    spaces = [pltpu.VMEM] * (len(arrays) - kept) + [pl.ANY] * kept
    aliases = {len(arrays) - kept + i: i for i in range(kept)}
    return kernel_call(
        kernel, arrays, spaces, shapes, scratch, "leaf_backward", out_space=pl.ANY, aliases=aliases
    )


def repacked(pieces, block_slot, parts, own_rows):
    planes, sep_rows = len(pieces), pieces[0].shape[-1]
    whole = jnp.concatenate(
        [lax.dynamic_index_in_dim(jnp.stack(pieces), block_slot[i], 0) for i in range(planes)], axis=0
    )
    count = planes * own_rows // LANES
    mats = whole[:, : parts * own_rows].reshape(count, planes // count, parts, own_rows, sep_rows)
    mats = jnp.transpose(mats, (0, 2, 1, 3, 4)).reshape(count, parts * LANES, sep_rows)
    rest = whole[:, parts * own_rows :, :own_rows]
    rest = rest.reshape(count, planes // count, rest.shape[1], own_rows)
    rest = jnp.transpose(rest, (0, 2, 1, 3)).reshape(count, rest.shape[2], LANES)
    rest = jnp.pad(rest, ((0, 0), (0, 0), (0, sep_rows - LANES)))
    mats = jnp.concatenate([mats, rest], axis=1)
    return [mats[i] for i in range(count)]


def body(
    leaf_rhs,
    leaf_inverse,
    leaf_couple,
    couple_mask,
    leaf_diag,
    sep_rhs,
    sep_inverse,
    sep_couple,
    sep_diag,
):
    levels = leaf_couple.shape[1]
    planes = lax.axis_size("plane")
    layers = lax.axis_size("layer")
    own_rows = sep_rhs.shape[1]

    own = collect_call(sep_inverse, sep_couple, sep_diag, levels, layers)
    mask = after(couple_mask.T, own[0])

    links = len(bit_orders(planes)[0])
    four = links == 2
    near = swap_link(own[0], links - 1) if four else own[0]
    quarter = planes // 4
    highs = [slot for slot in range(planes) if slot // quarter % 2 == 1]
    lows = [slot for slot in range(planes) if slot // quarter % 2 == 0]
    leaf_y, keep, *send = leaf_forward_call(
        mask, [leaf_rhs, leaf_inverse], leaf_couple, sep_rhs, highs, layers, True
    )
    own_crossed = [swap_core(own[0])] if four else []
    high = [joined_call(keep, [swap_core(part) for part in send], own_crossed)]
    keep, send = leaf_forward_call(mask, [leaf_y], leaf_couple, sep_rhs, lows, layers, False)
    low = [keep, swap_core(send)]
    parts, arrived = scatter_sum(low, high)
    seen = []

    def fitted(pieces, level):
        if own_rows == LANES:
            return pieces
        me = lax.axis_index("plane")
        parity = jnp.bitwise_and(jnp.bitwise_xor(me, lax.axis_index("layer")), 1)
        slots = jnp.bitwise_xor(me, jnp.asarray([slot_table(planes, 0), slot_table(planes, 1)])[parity])
        return repacked(pieces, jnp.argsort(slots).astype(jnp.int32), 1 + levels - level, own_rows)

    if four:
        near_crossed = swap_core(after(near, arrived[0]))
        side = swap_layer(near, 0)
        far = swap_link(near, 0)
        last_own = after(own[-1], arrived[0])
        last_near = swap_link(last_own, 1)
        parts[0] = after(parts[0], near_crossed)
        seen = [seen_call(side, 3_000_000_000)]
        last = [own[-1], last_near, swap_link(after(last_own, arrived[1]), 0)]
    else:
        first = gather(own[0])
    far_seen = [seen_call(far, 6_000_000_000)] if four else []
    sums = first_call(parts, seen, 1)
    groups, solved = [], []
    for level in range(1, levels + 1):
        theirs = swap_layer(sums, level - 1)
        if four and level == 1:
            theirs = after(theirs, last_near)
        sums = added_call(sums, theirs, far_seen, 4_000_000_000) if level == 1 else added(sums, theirs)
        if level == 1:
            if four:
                first = [own[0], near, side, far, own_crossed[0], near_crossed, swap_core(side), swap_core(far)]
            groups.append(fitted(first, 1))
        elif four and level == levels:
            groups.append(fitted(last + [swap_core(piece) for piece in last[2:4]], level))
        else:
            groups.append(fitted(gather(own[level - 1]), level))
        if level < levels:
            y, sums = level_forward_call(planes, sums, groups[level - 1])
            solved.append(y)
        if level == 1 and four:
            last = last + [swap_link(last_near, 0), *[swap_core(piece) for piece in after_all([last[0], last_near], y)]]
    answers = backward_call(planes, sums, solved, groups)
    leaves = [mask, leaf_y, leaf_inverse, leaf_couple, leaf_diag]
    if not four or 2 * answers.shape[1] != LANES:
        above = dict(enumerate(gather(answers)))
        return tuple(leaf_backward_call(*leaves, above, [list(range(planes))], [], own_rows))
    above = dict(enumerate(gather(answers, cross=False)))
    for slot in range(3):
        above[4 + slot] = swap_core(above[slot])
    early = leaf_backward_call(*leaves, above, [[0, 4], [1, 6], [2, 5]], [], own_rows)
    above[7] = swap_core(after(above[3], early[0]))
    return tuple(leaf_backward_call(*leaves, above, [[3, 7]], early, own_rows))


def solution(mesh):
    in_specs = (
        P(("layer", "plane"), None, None),
        P(("layer", "plane"), None, None),
        P(("layer", "plane"), None, None, None),
        P(("layer", "plane"), None),
        P(("layer", "plane"), None),
        P(None, "plane", None),
        P(None, "plane", None),
        P(None, None, "plane", None),
        P(None, "plane"),
    )
    out_specs = (P(("layer", "plane"), None, None), P("layer", None, "plane", None))
    return jax.shard_map(body, mesh=mesh, in_specs=in_specs, out_specs=out_specs, check_vma=False)
```

```python
import jax
import jax.numpy as jnp
from jax import lax
from jax.experimental import pallas as pl
from jax.experimental.pallas import tpu as pltpu
from jax.sharding import PartitionSpec as P

F32 = jnp.float32
BF16 = jnp.bfloat16
LANES = 128
TILE = 256
DIAG_ROWS = 16
NT = (((1,), (1,)), ((), ()))
VMEM = pltpu.CompilerParams(vmem_limit_bytes=32 * 1024 * 1024)


def bit_orders(planes):
    link_bits = list(range(1, planes.bit_length() - 1))
    turn = len(link_bits) // 2
    return [link_bits, link_bits[turn:] + link_bits[:turn]]


def slot_table(planes, parity):
    orders = bit_orders(planes)
    count = len(orders[0])
    table = []
    for slot in range(planes):
        other = slot >> count
        block = other
        for place, bit in enumerate(orders[parity ^ other]):
            if slot >> (count - 1 - place) & 1:
                block ^= 1 << bit
        table.append(block)
    return table


def swap_core(value):
    planes = lax.axis_size("plane")
    return lax.ppermute(value, "plane", [(i, i ^ 1) for i in range(planes)])


def swap_link(value, place):
    planes, layers = lax.axis_size("plane"), lax.axis_size("layer")
    orders = bit_orders(planes)
    pairs = []
    for layer in range(layers):
        for i in range(planes):
            bit = orders[(i ^ layer) & 1][place]
            pairs.append((layer * planes + i, layer * planes + (i ^ (1 << bit))))
    return lax.ppermute(value, ("layer", "plane"), pairs)


def swap_layer(value, stride):
    layers = lax.axis_size("layer")
    return lax.ppermute(value, "layer", [(i, i ^ (1 << stride)) for i in range(layers)])


def after(value, *others):
    return lax.optimization_barrier((value, *others))[0]


def after_all(values, *others):
    return lax.optimization_barrier((*values, *others))[: len(values)]


def added(*terms):
    total = terms[0].astype(F32)
    for term in terms[1:]:
        total = total + term.astype(F32)
    return total.astype(BF16)


def scatter_sum(low, high):
    parts = list(low)
    for place in range(len(bit_orders(lax.axis_size("plane"))[0])):
        parts.append(swap_link(added(*high), place))
        low = [*low, parts[-1]]
        half = low[0].shape[0] // 2
        low, high = [term[:half] for term in low], [term[half:] for term in low]
    return parts, parts[-len(bit_orders(lax.axis_size("plane"))[0]) :]


def gather(value, cross=True):
    pieces = [value]
    for place in reversed(range(len(bit_orders(lax.axis_size("plane"))[0]))):
        pieces = pieces + [swap_link(piece, place) for piece in pieces]
    return pieces + [swap_core(piece) for piece in pieces] if cross else pieces


def lower_unit(block, first_row):
    row_count = block.shape[-2]
    col_count = block.shape[-1]
    row_ids = first_row + lax.broadcasted_iota(jnp.int32, (row_count, col_count), 0)
    col_ids = lax.broadcasted_iota(jnp.int32, (row_count, col_count), 1)
    below = jnp.where(col_ids < row_ids, block, jnp.zeros_like(block))
    return jnp.where(col_ids == row_ids, jnp.ones_like(block), below)


def nt(left, right):
    return lax.dot_general(left, right, NT, preferred_element_type=F32)


def nn(left, right):
    return jnp.dot(left, right, preferred_element_type=F32)


def places():
    return lax.axis_index("plane").astype(jnp.int32), lax.axis_index("layer").astype(jnp.int32)


def slot_blocks(planes):
    me, layer_id = places()
    parity = jnp.bitwise_and(jnp.bitwise_xor(me, layer_id), 1)
    even, odd = slot_table(planes, 0), slot_table(planes, 1)
    return [jnp.bitwise_xor(me, even[i] + parity * (odd[i] - even[i])) for i in range(planes)]


def at_multiple(index, size):
    return pl.ds(pl.multiple_of(index * size, size), size)


def sep_index(layer_id, level, layers):
    return layers - (layers >> level - 1) + jnp.right_shift(layer_id, level)


def kernel_call(kernel, arrays, spaces, out_shapes, scratch, name, flops=1, out_space=pltpu.VMEM, aliases={}):
    arrays = [
        pltpu.with_memory_space_constraint(array, space) if space == pltpu.HBM else array
        for array, space in zip(arrays, spaces)
    ]
    return pl.pallas_call(
        kernel,
        in_specs=[pl.BlockSpec(memory_space=space) for space in spaces],
        out_specs=[pl.BlockSpec(memory_space=out_space)] * len(out_shapes),
        out_shape=out_shapes,
        scratch_shapes=scratch,
        input_output_aliases=aliases,
        compiler_params=VMEM,
        cost_estimate=pl.CostEstimate(flops=flops, bytes_accessed=1, transcendentals=0),
        name=name,
    )(*arrays)


def collect_call(sep_inverse, sep_couple, sep_diag, levels, layers):
    own_rows, sep_rows = sep_inverse.shape[1:]

    def kernel(inverse, couple, diag_in, *refs):
        outs, (held, diag, sems, couple_sems) = refs[:levels], refs[levels:]
        me, layer_id = places()
        diag_load = pltpu.make_async_copy(diag_in, diag, sems.at[levels])
        diag_load.start()
        loads, moves = [], []
        for level in range(1, levels + 1):
            sep = sep_index(layer_id, level, layers)
            loads.append(pltpu.make_async_copy(inverse.at[sep], held.at[level - 1], sems.at[level - 1]))
            loads[-1].start()
            for slot in range(levels - level):
                rows = slice((slot + 1) * own_rows, (slot + 2) * own_rows)
                moves.append(
                    pltpu.make_async_copy(
                        couple.at[sep, slot], outs[level - 1].at[rows], couple_sems.at[level - 1, slot]
                    )
                )
                moves[-1].start()
        diag_load.wait()
        rows = []
        for level in range(1, levels + 1):
            value = diag[pl.ds(sep_index(layer_id, level, layers), 1)]
            high = value.astype(BF16).astype(F32)
            rows += [high, value - high]
        rows.append(jnp.zeros((DIAG_ROWS - len(rows), own_rows), F32))
        outs[-1][own_rows:] = jnp.zeros((DIAG_ROWS, sep_rows), BF16)
        outs[-1][own_rows:, :own_rows] = jnp.concatenate(rows, axis=0).astype(BF16)
        for level in range(1, levels + 1):
            loads[level - 1].wait()
            lower = lower_unit(held[level - 1].astype(F32), me * own_rows)
            outs[level - 1][:own_rows] = lower.astype(BF16)
        for move in moves:
            move.wait()

    shapes = [((1 + levels - level) * own_rows, sep_rows) for level in range(1, levels + 1)]
    shapes[-1] = (own_rows + DIAG_ROWS, sep_rows)
    return kernel_call(
        kernel,
        [sep_inverse, sep_couple, sep_diag],
        [pltpu.HBM] * 3,
        [jax.ShapeDtypeStruct(shape, BF16) for shape in shapes],
        [
            pltpu.VMEM((levels, own_rows, sep_rows), BF16),
            pltpu.VMEM(sep_diag.shape, F32),
            pltpu.SemaphoreType.DMA((levels + 1,)),
            pltpu.SemaphoreType.DMA((levels, levels)),
        ],
        "collect",
        flops=20_000_000_000,
    )


def leaf_forward_call(mask, leaves, couple, sep_rhs, slots, layers, apart):
    first = apart
    blocks, levels, sep_rows, block_rows = couple.shape
    own_rows, rhs_cols = sep_rhs.shape[1:]
    planes = sep_rows // own_rows
    cols = rhs_cols // planes
    here = len(slots) * cols
    width = blocks * block_rows
    tile = min(TILE, sep_rows)
    tiles = sep_rows // tile

    def kernel(mask, *refs):
        if first:
            rhs, inverse, couple, own_rhs, y, *parts, scaled, turned = refs
        else:
            y, inverse, couple, own_rhs, lower_turned, *parts, scaled, turned = refs
            for b in range(blocks):
                lower_turned[b] = lower_unit(inverse[b].astype(F32), 0).T.astype(BF16)
        me, layer_id = places()
        order = slot_blocks(planes)
        if first:
            for b in range(blocks):
                lower = lower_unit(inverse[b].astype(F32), 0).astype(BF16)
                y[:, b * block_rows : (b + 1) * block_rows] = nn(lower, rhs[b]).T.astype(BF16)
        for level in range(levels):
            alone = (jnp.bitwise_and(layer_id, (2 << level) - 1) == 0).astype(F32)
            own = own_rhs[sep_index(layer_id, level + 1, layers)].astype(F32)
            turned[...] = (own.T * -alone).astype(BF16)
            for at, slot in enumerate(slots):
                rows = slice(at * cols, (at + 1) * cols)
                scaled[level, rows, width:] = turned[at_multiple(order[slot], cols)]
                for b in range(blocks):
                    place = slice(b * block_rows, (b + 1) * block_rows)
                    used = mask[level : level + 1, b : b + 1].astype(F32).astype(BF16)
                    scaled[level, rows, place] = y[at_multiple(order[slot], cols), place] * used
        for level in range(levels):
            for t in range(tiles):
                lanes = slice(t * tile, (t + 1) * tile)
                row_ids = t * tile + lax.broadcasted_iota(jnp.int32, (tile, own_rows), 0)
                own_ids = me * own_rows + lax.broadcasted_iota(jnp.int32, (tile, own_rows), 1)
                chosen = (row_ids == own_ids).astype(F32).astype(BF16)
                weights = jnp.concatenate([couple[b, level, lanes] for b in range(blocks)] + [chosen], axis=1)
                total = nt(scaled[level], weights).astype(BF16)
                half = len(slots) // 2
                for at in range(len(slots)):
                    value = total[at * cols : (at + 1) * cols]
                    if at < half:
                        parts[0][at, level, :, lanes] = value
                    elif apart:
                        parts[1 + level][at - half, :, lanes] = value
                    else:
                        parts[1][at - half, level, :, lanes] = value

    part = jax.ShapeDtypeStruct((len(slots) // 2, levels, cols, sep_rows), BF16)
    y_shape = [jax.ShapeDtypeStruct((rhs_cols, width) if first else leaves[1].shape, BF16)]
    scratch = [pltpu.VMEM((levels, here, width + own_rows), BF16), pltpu.VMEM((rhs_cols, own_rows), BF16)]
    arrays = [mask, *leaves, couple, sep_rhs]
    one = jax.ShapeDtypeStruct((len(slots) // 2, cols, sep_rows), BF16)
    sent = [one] * levels if apart else [part]
    return vmem_call(kernel, arrays, [*y_shape, part, *sent], scratch, "leaf_forward")


def joined_call(kept, others, seen):
    def kernel(kept, *refs):
        for level, other in enumerate(refs[: len(others)]):
            refs[-1][:, level] = (kept[:, level].astype(F32) + other[...].astype(F32)).astype(BF16)

    return vmem_call(kernel, [kept, *others, *seen], [jax.ShapeDtypeStruct(kept.shape, BF16)], [], "joined")[0]


def first_call(parts, seen, flops):
    def kernel(*refs):
        total = refs[0][0].astype(F32)
        for ref in refs[1 : len(parts)]:
            total = total + ref[0].astype(F32)
        refs[-1][...] = total.astype(BF16)

    shapes = [jax.ShapeDtypeStruct(parts[0].shape[1:], BF16)]
    arrays = [*parts, *seen]
    return kernel_call(kernel, arrays, [pltpu.VMEM] * len(arrays), shapes, [], "first", flops)[0]


def seen_call(value, flops):
    rows, lanes = min(DIAG_ROWS, value.shape[0]), min(LANES, value.shape[1])

    def kernel(value, out):
        out[...] = value[:rows, :lanes]

    shapes = [jax.ShapeDtypeStruct((rows, lanes), BF16)]
    return kernel_call(kernel, [value], [pltpu.VMEM], shapes, [], "seen", flops)[0]


def added_call(ours, theirs, seen, flops):
    def kernel(ours, theirs, *refs):
        refs[-1][...] = (ours[...].astype(F32) + theirs[...].astype(F32)).astype(BF16)

    arrays = [ours, theirs, *seen]
    shapes = [jax.ShapeDtypeStruct(ours.shape, BF16)]
    return kernel_call(kernel, arrays, [pltpu.VMEM] * len(arrays), shapes, [], "added", flops)[0]


def paired(count):
    step = 2 if count % 2 == 0 else 1
    return [range(i, i + step) for i in range(0, count, step)]


def rows_times(pieces, part, vector, out, order):
    for group in paired(len(pieces)):
        rows = jnp.concatenate([pieces[i][part] for i in group], axis=0)
        result = nt(vector, rows)
        for at, i in enumerate(group):
            lanes = pl.ds(pl.multiple_of(order[i] * LANES, LANES), LANES)
            out[:, lanes] = result[:, at * LANES : (at + 1) * LANES].astype(out.dtype)


def times_rows(pieces, part, vector, order):
    total = None
    for group in paired(len(pieces)):
        rows = jnp.concatenate([pieces[i][part] for i in group], axis=0)
        left = jnp.concatenate(
            [vector[:, pl.ds(pl.multiple_of(order[i] * LANES, LANES), LANES)] for i in group], axis=1
        ).astype(BF16)
        term = nn(left, rows)
        total = term if total is None else total + term
    return total


def at_part(index):
    return slice(index * LANES, (index + 1) * LANES)


def vmem_call(kernel, arrays, out_shapes, scratch, name):
    return kernel_call(kernel, arrays, [pltpu.VMEM] * len(arrays), out_shapes, scratch, name)


def piece_order(count, planes):
    return slot_blocks(planes) if count == planes else list(range(count))


def level_forward_call(planes, sums, pieces):
    count = len(pieces)
    levels = sums.shape[0]

    def kernel(sums, *refs):
        order = piece_order(count, planes)
        pieces, (y, outs, work) = refs[:count], refs[count:]
        rows_times(pieces, at_part(0), -sums[0], y, order)
        for level in range(1, levels):
            rows_times(pieces, at_part(level), y[...], work, order)
            outs[level - 1] = (sums[level].astype(F32) + work[...]).astype(BF16)

    shape = sums.shape[1:]
    shapes = [jax.ShapeDtypeStruct(shape, BF16), jax.ShapeDtypeStruct((levels - 1, *shape), BF16)]
    return vmem_call(kernel, [sums, *pieces], shapes, [pltpu.VMEM(shape, F32)], "level_forward")


def backward_call(planes, sums, solved, groups):
    levels = len(groups)
    count = len(groups[0])
    lower = levels - 1

    def kernel(sums, *refs):
        order = piece_order(count, planes)
        solved, refs = refs[:lower], refs[lower:]
        pieces, (out, diag, work) = [refs[i * count : (i + 1) * count] for i in range(levels)], refs[-3:]
        for i in range(count):
            split = pieces[-1][i][LANES : LANES + DIAG_ROWS, :LANES].astype(F32)
            for level in range(levels):
                value = split[2 * level : 2 * level + 1] + split[2 * level + 1 : 2 * level + 2]
                diag[level : level + 1, at_multiple(order[i], LANES)] = value
        rows_times(pieces[-1], at_part(0), -sums[0], work, order)
        for level in range(levels, 0, -1):
            y = work if level == levels else solved[level - 1]
            value = y[...].astype(F32) / diag[level - 1 : level]
            for slot in range(levels - level):
                upper = out.at[level + slot]
                value = value - times_rows(pieces[level - 1], at_part(slot + 1), upper, order)
            work[...] = value.astype(BF16)
            out[level - 1] = times_rows(pieces[level - 1], at_part(0), work, order).astype(BF16)

    arrays = [sums, *solved, *[piece for group in groups for piece in group]]
    shape = sums.shape[1:]
    shapes = [jax.ShapeDtypeStruct((levels, *shape), BF16)]
    scratch = [pltpu.VMEM((levels, shape[1]), F32), pltpu.VMEM(shape, BF16)]
    return vmem_call(kernel, arrays, shapes, scratch, "backward")[0]


def leaf_backward_call(mask, y, turned, couple, diag, above, groups, before, own_rows):
    blocks, levels, sep_rows, block_rows = couple.shape
    rhs_cols, width = y.shape
    planes = sep_rows // own_rows
    cols = rhs_cols // planes
    slots = [slot for group in groups for slot in group]
    size = len(groups[0]) * cols
    here = len(slots) * cols
    pair = 2 if blocks % 2 == 0 else 1
    steps = blocks // pair
    kept = len(before)

    def kernel(mask, y, turned, couple, diag, *refs):
        pieces, refs = dict(zip(slots, refs)), refs[len(slots) + kept :]
        leaf_to, sep_to, whole, ys, leaf_out, sep_out, sems = refs
        me = places()[0]
        order = slot_blocks(planes)
        stores = []

        def store(source, target):
            stores.append(pltpu.make_async_copy(source, target, sems.at[len(stores)]))
            stores[-1].start()

        lanes = []
        for j, group in enumerate(groups):
            lanes.append(at_multiple(order[group[0]] // len(group), size))
            rows = slice(j * size, (j + 1) * size)
            ys[rows] = y[lanes[j]]
            for slot in group:
                row = j * size + lax.rem(order[slot], len(group)) * cols
                for level in range(levels):
                    whole[level, pl.ds(pl.multiple_of(row, cols), cols)] = pieces[slot][level]
        row_ids = me * own_rows + lax.broadcasted_iota(jnp.int32, (own_rows, sep_rows), 0)
        col_ids = lax.broadcasted_iota(jnp.int32, (own_rows, sep_rows), 1)
        chosen = (row_ids == col_ids).astype(F32).astype(BF16)
        for level in range(levels):
            sep_out[level] = nt(chosen, whole[level]).astype(BF16)
            for j in range(len(groups)):
                store(sep_out.at[level, :, j * size : (j + 1) * size], sep_to.at[0, level, :, lanes[j]])
        for step in range(steps):
            terms = [None] * pair
            for level in range(levels):
                weights = jnp.concatenate([couple[step * pair + b, level] for b in range(pair)], axis=1)
                value = nn(whole[level], weights)
                for b in range(pair):
                    place = slice(b * block_rows, (b + 1) * block_rows)
                    at = step * pair + b
                    term = value[:, place] * mask[level : level + 1, at : at + 1].astype(F32)
                    terms[b] = term if terms[b] is None else terms[b] + term
            for b in range(pair):
                at = step * pair + b
                place = slice(at * block_rows, (at + 1) * block_rows)
                scale = 1.0 / diag[at : at + 1]
                target = (ys[:, place].astype(F32) * scale - terms[b]).astype(BF16)
                leaf_out[at] = nt(turned[at], target).astype(BF16)
            at = slice(step * pair, (step + 1) * pair)
            for j in range(len(groups)):
                store(leaf_out.at[at, :, j * size : (j + 1) * size], leaf_to.at[at, :, lanes[j]])
        for copy in stores:
            copy.wait()

    arrays = [mask, y, turned, couple, diag, *[above[slot] for slot in slots], *before]
    shapes = [
        jax.ShapeDtypeStruct((blocks, block_rows, rhs_cols), BF16),
        jax.ShapeDtypeStruct((1, levels, own_rows, rhs_cols), BF16),
    ]
    scratch = [
        pltpu.VMEM((levels, here, sep_rows), BF16),
        pltpu.VMEM((here, width), BF16),
        pltpu.VMEM((blocks, block_rows, here), BF16),
        pltpu.VMEM((levels, own_rows, here), BF16),
        pltpu.SemaphoreType.DMA(((levels + steps) * len(groups),)),
    ]
    spaces = [pltpu.VMEM] * (len(arrays) - kept) + [pl.ANY] * kept
    aliases = {len(arrays) - kept + i: i for i in range(kept)}
    return kernel_call(
        kernel, arrays, spaces, shapes, scratch, "leaf_backward", out_space=pl.ANY, aliases=aliases
    )


def repacked(pieces, block_slot, parts, own_rows):
    planes, sep_rows = len(pieces), pieces[0].shape[-1]
    whole = jnp.concatenate(
        [lax.dynamic_index_in_dim(jnp.stack(pieces), block_slot[i], 0) for i in range(planes)], axis=0
    )
    count = planes * own_rows // LANES
    mats = whole[:, : parts * own_rows].reshape(count, planes // count, parts, own_rows, sep_rows)
    mats = jnp.transpose(mats, (0, 2, 1, 3, 4)).reshape(count, parts * LANES, sep_rows)
    rest = whole[:, parts * own_rows :, :own_rows]
    rest = rest.reshape(count, planes // count, rest.shape[1], own_rows)
    rest = jnp.transpose(rest, (0, 2, 1, 3)).reshape(count, rest.shape[2], LANES)
    rest = jnp.pad(rest, ((0, 0), (0, 0), (0, sep_rows - LANES)))
    mats = jnp.concatenate([mats, rest], axis=1)
    return [mats[i] for i in range(count)]


def body(
    leaf_rhs,
    leaf_inverse,
    leaf_couple,
    couple_mask,
    leaf_diag,
    sep_rhs,
    sep_inverse,
    sep_couple,
    sep_diag,
):
    levels = leaf_couple.shape[1]
    planes = lax.axis_size("plane")
    layers = lax.axis_size("layer")
    own_rows = sep_rhs.shape[1]

    own = collect_call(sep_inverse, sep_couple, sep_diag, levels, layers)
    mask = after(couple_mask.T, own[0])

    links = len(bit_orders(planes)[0])
    four = links == 2
    near = swap_link(own[0], links - 1) if four else own[0]
    quarter = planes // 4
    highs = [slot for slot in range(planes) if slot // quarter % 2 == 1]
    lows = [slot for slot in range(planes) if slot // quarter % 2 == 0]
    leaf_y, keep, *send = leaf_forward_call(
        mask, [leaf_rhs, leaf_inverse], leaf_couple, sep_rhs, highs, layers, True
    )
    own_crossed = [swap_core(own[0])] if four else []
    high = [joined_call(keep, [swap_core(part) for part in send], own_crossed)]
    turned, keep, send = leaf_forward_call(mask, [leaf_y, leaf_inverse], leaf_couple, sep_rhs, lows, layers, False)
    low = [keep, swap_core(send)]
    parts, arrived = scatter_sum(low, high)
    seen = []

    def fitted(pieces, level):
        if own_rows == LANES:
            return pieces
        me = lax.axis_index("plane")
        parity = jnp.bitwise_and(jnp.bitwise_xor(me, lax.axis_index("layer")), 1)
        slots = jnp.bitwise_xor(me, jnp.asarray([slot_table(planes, 0), slot_table(planes, 1)])[parity])
        return repacked(pieces, jnp.argsort(slots).astype(jnp.int32), 1 + levels - level, own_rows)

    if four:
        near_crossed = swap_core(after(near, arrived[0]))
        side = swap_layer(near, 0)
        far = swap_link(near, 0)
        last_own = after(own[-1], arrived[0])
        last_near = swap_link(last_own, 1)
        parts[0] = after(parts[0], near_crossed)
        seen = [seen_call(side, 3_000_000_000)]
        last = [own[-1], last_near, swap_link(after(last_own, arrived[1]), 0)]
    else:
        first = gather(own[0])
    far_seen = [seen_call(far, 6_000_000_000)] if four else []
    sums = first_call(parts, seen, 1)
    groups, solved = [], []
    for level in range(1, levels + 1):
        theirs = swap_layer(sums, level - 1)
        if four and level == 1:
            theirs = after(theirs, last_near)
        sums = added_call(sums, theirs, far_seen, 4_000_000_000) if level == 1 else added(sums, theirs)
        if level == 1:
            if four:
                first = [own[0], near, side, far, own_crossed[0], near_crossed, swap_core(side), swap_core(far)]
            groups.append(fitted(first, 1))
        elif four and level == levels:
            groups.append(fitted(last + [swap_core(piece) for piece in last[2:4]], level))
        else:
            groups.append(fitted(gather(own[level - 1]), level))
        if level < levels:
            y, sums = level_forward_call(planes, sums, groups[level - 1])
            solved.append(y)
        if level == 1 and four:
            last = last + [swap_link(last_near, 0), *[swap_core(piece) for piece in after_all([last[0], last_near], y)]]
    answers = backward_call(planes, sums, solved, groups)
    leaves = [mask, leaf_y, turned, leaf_couple, leaf_diag]
    if not four or 2 * answers.shape[1] != LANES:
        above = dict(enumerate(gather(answers)))
        return tuple(leaf_backward_call(*leaves, above, [list(range(planes))], [], own_rows))
    above = dict(enumerate(gather(answers, cross=False)))
    for slot in range(3):
        above[4 + slot] = swap_core(above[slot])
    early = leaf_backward_call(*leaves, above, [[0, 4], [1, 6], [2, 5]], [], own_rows)
    above[7] = swap_core(after(above[3], early[0]))
    return tuple(leaf_backward_call(*leaves, above, [[3, 7]], early, own_rows))


def solution(mesh):
    in_specs = (
        P(("layer", "plane"), None, None),
        P(("layer", "plane"), None, None),
        P(("layer", "plane"), None, None, None),
        P(("layer", "plane"), None),
        P(("layer", "plane"), None),
        P(None, "plane", None),
        P(None, "plane", None),
        P(None, None, "plane", None),
        P(None, "plane"),
    )
    out_specs = (P(("layer", "plane"), None, None), P("layer", None, "plane", None))
    return jax.shard_map(body, mesh=mesh, in_specs=in_specs, out_specs=out_specs, check_vma=False)
```
